256 devices in a mesh: section: 32 (over x, z), tensor: 4 (over y_hi, core), dp: 2 (over y_lo).
Axes of the slice: x: 4, y: 4 (y_hi: 2, y_lo: 2; y = y_hi * 2 + y_lo), z: 8, core: 2. Of those that a mesh axis runs over, the one named last changes fastest.
Arguments:
- grad_in: bfloat16 [32, 512, 2560], P('section', 'dp', 'tensor'), parts along dimension 1, may hold values from -6 to 6
- grad_top: bfloat16 [1, 512, 2560], P(None, 'dp', 'tensor'), parts along dimension 1, may hold values from -6 to 6
- queries: bfloat16 [32, 2, 512, 2560], P('section', None, 'dp', 'tensor'), parts along dimension 2, may hold values from -80 to 80
- keys: bfloat16 [32, 1024, 2560], P('section', 'dp', 'tensor'), parts along dimension 1, may hold values from -4 to 4
- values: bfloat16 [32, 1024, 2560], P('section', 'dp', 'tensor'), parts along dimension 1, may hold values from -4 to 4
- query_weight: bfloat16 [32, 2560, 2560], P('section', None, 'tensor'), may hold values from -0.75 to 0.75
- key_weight: bfloat16 [32, 2560, 2560], P('section', None, 'tensor'), may hold values from -0.125 to 0.125
- value_weight: bfloat16 [32, 2560, 2560], P('section', None, 'tensor'), may hold values from -0.125 to 0.125
- text_weight: bfloat16 [2560, 2560], P('section', 'tensor'), may hold values from -0.125 to 0.125
- text_hidden: bfloat16 [2560, 1024], P('tensor', ('dp', 'section')), parts along dimension 1, may hold values from -5 to 5
Outputs:
- sent: bfloat16 [32, 2, 512, 2560], P('section', None, 'dp', 'tensor'), parts along dimension 2
- text_grad: float32 [2560, 1024], P('tensor', ('dp', 'section')), parts along dimension 1
The draws below stay inside these ranges and needn't reach their ends.
There are 2 independent parts, one for each index of `dp`. The reference program is written for one: setup_inputs(seed, part) draws one part's arguments, and reference() takes and returns one part's arrays. A program takes and returns all parts, laid end to end along the dimension named above; an argument that names none is the same for every part. Nothing has to cross between parts.
All inputs are finite; a program needn't handle non-finite values.
Results may differ from the reference program's by a relative error of at most 0.03.
Values may be sent and summed in bfloat16 or wider, within the bound.
No kernel may reach another device: no remote copies, remote signals or barrier semaphores. Data moves between devices by JAX's collectives and lax.ppermute only.
A program may use at most 64 MiB of HBM per device.

```python
import jax
import jax.numpy as jnp
from jax import lax

HEADS = 20
HEAD_DIM = 128
D = 2560
HID = 2560
CTX = 512
BLOCK = 256
TICKS = 2
N_SECTION = 32
N_TENSOR = 4


def shared_keys(key):
    return jnp.clip(jax.random.normal(jax.random.fold_in(key, 7), (N_SECTION, CTX, D), jnp.float32), -4.0, 4.0)


def draw_keys(key, part):
    base = shared_keys(key)
    return base.astype(jnp.bfloat16)


def draw_queries(key, part):
    key = jax.random.fold_in(key, 3)
    query_rows = jnp.clip(jax.random.normal(key, (N_SECTION, TICKS, BLOCK, D), jnp.float32), -4.0, 4.0)
    return query_rows.astype(jnp.bfloat16)


def shard_levels(stream_key, dims, pieces, low, high):
    def one(dim, parts):
        draws = jax.random.uniform(jax.random.fold_in(jax.random.fold_in(stream_key, 6), dim), (parts,), jnp.float32, low / len(pieces), high / len(pieces))
        return jnp.repeat(jnp.exp(draws), dims[dim] // parts).reshape((-1,) + (1,) * (len(dims) - dim - 1))

    loudness = one(*pieces[0])
    for cut in pieces[1:]:
        loudness = loudness * one(*cut)
    return loudness


def centred(own_key, extent, deviation, bound, shards=(), dtype=jnp.bfloat16):
    entries = deviation * jax.random.normal(own_key, extent, jnp.float32)
    if shards:
        entries = entries * shard_levels(own_key, extent, shards, -0.22, 0.18)
    return jnp.clip(entries, -bound, bound).astype(dtype)


def setup_inputs(seed: int = 0, part: int = 0) -> dict:
    seeds = jax.random.split(jax.random.key(seed), 11)
    own_keys = jax.random.split(jax.random.fold_in(seeds[10], part), 11)
    grad_in = centred(own_keys[0], (N_SECTION, BLOCK, D), 1.0, 6.0, ((0, 32), (2, 4)))
    grad_top = centred(own_keys[1], (TICKS - 1, BLOCK, D), 1.0, 6.0, ((2, 4),))
    queries = draw_queries(jax.random.fold_in(jax.random.fold_in(seeds[10], part), 71), part)
    keys = draw_keys(jax.random.fold_in(jax.random.fold_in(seeds[10], part), 71), part)
    values = centred(own_keys[4], (N_SECTION, CTX, D), 1.0, 4.0, ((0, 32), (2, 4)))
    query_weight = centred(seeds[5], (N_SECTION, D, D), 64 ** -0.5, 0.75, ((0, 32), (2, 4)))
    key_weight = centred(seeds[6], (N_SECTION, D, D), D ** -0.5, 0.125, ((0, 32), (2, 4)))
    value_weight = centred(seeds[7], (N_SECTION, D, D), D ** -0.5, 0.125, ((0, 32), (2, 4)))
    text_weight = centred(seeds[8], (HID, D), HID ** -0.5, 0.125, ((0, 32), (1, 4)))
    text_hidden = centred(own_keys[9], (HID, CTX), 1.0, 5.0, ((0, 4), (1, 32)))
    return dict(grad_in=grad_in, grad_top=grad_top, queries=queries, keys=keys, values=values, query_weight=query_weight, key_weight=key_weight, value_weight=value_weight, text_weight=text_weight, text_hidden=text_hidden)


def smooth_gate(inputs):
    return jax.nn.gelu(inputs, approximate=True)

def gelu_slope(inputs):
    unused_out, backward = jax.vjp(smooth_gate, inputs)
    return backward(jnp.ones_like(inputs))[0]

def attention_back(query_rows, key_rows, value_rows, grad_rows, head_count, head_width):
    token_count = query_rows.shape[0]
    context_count = key_rows.shape[0]
    query_heads = query_rows.astype(jnp.float32).reshape(token_count, head_count, head_width)
    key_heads = key_rows.astype(jnp.float32).reshape(context_count, head_count, head_width)
    value_heads = value_rows.astype(jnp.float32).reshape(context_count, head_count, head_width)
    grad_heads = grad_rows.astype(jnp.float32).reshape(token_count, head_count, head_width)
    scale_factor = head_width ** (-0.5)
    scores = jnp.einsum('qhd,chd->hqc', query_heads, key_heads) * scale_factor
    peak = lax.optimization_barrier(jnp.max(scores, axis=-1, keepdims=True))
    shifted = jnp.exp(scores - peak)
    attention = shifted / lax.optimization_barrier(jnp.sum(shifted, axis=-1, keepdims=True))
    attention_low = lax.optimization_barrier(attention.astype(jnp.bfloat16)).astype(jnp.float32)
    attention_grad = jnp.einsum('qhd,chd->hqc', grad_heads, value_heads)
    row_dot = lax.optimization_barrier(jnp.sum(attention * attention_grad, axis=-1, keepdims=True))
    score_grad = lax.optimization_barrier((attention * (attention_grad - row_dot)).astype(jnp.bfloat16)).astype(jnp.float32)
    query_grad = (jnp.einsum('hqc,chd->qhd', score_grad, key_heads) * scale_factor).astype(jnp.bfloat16)
    key_grad = jnp.einsum('hqc,qhd->chd', score_grad, query_heads) * scale_factor
    value_grad = jnp.einsum('hqc,qhd->chd', attention_low, grad_heads)
    return (query_grad.reshape(token_count, head_count * head_width), key_grad.reshape(context_count, head_count * head_width), value_grad.reshape(context_count, head_count * head_width))

def split_groups(matrix, part_width):
    return matrix.astype(jnp.float32).reshape(matrix.shape[0], N_TENSOR, part_width)

def reference(grad_in, grad_top, queries, keys, values, query_weight, key_weight, value_weight, text_weight, text_hidden):
    part_width = D // N_TENSOR

    def section_step(operands):
        query_rows, key_rows, value_rows, grad_rows, weight_rows = operands
        query_grad, key_grad, value_grad = attention_back(query_rows, key_rows, value_rows, grad_rows, HEADS, HEAD_DIM)
        head_terms = jnp.einsum('qtk,dtk->tqd', split_groups(query_grad, part_width), split_groups(weight_rows, part_width))
        rounded = lax.optimization_barrier(head_terms.astype(jnp.bfloat16)).astype(jnp.float32)
        outgoing = (grad_rows.astype(jnp.float32) + lax.optimization_barrier(jnp.sum(rounded, axis=0))).astype(jnp.bfloat16)
        return (outgoing, key_grad, value_grad)
    incoming = grad_in
    outgoing = grad_in
    key_total = jnp.zeros((N_SECTION, CTX, D), jnp.float32)
    value_total = jnp.zeros((N_SECTION, CTX, D), jnp.float32)
    sent_list = []
    for step_index in range(TICKS):
        if step_index > 0:
            incoming = jnp.concatenate([outgoing[1:], grad_top[step_index - 1][None]], axis=0)
        outgoing, key_grad, value_grad = lax.map(section_step, (queries[:, step_index], keys, values, incoming, query_weight))
        key_total = key_total + key_grad
        value_total = value_total + value_grad
        sent_list.append(outgoing)
    sent = jnp.stack(sent_list, axis=1)

    def context_step(operands):
        key_rows, value_rows, key_sums, value_sums = operands
        key_low = lax.optimization_barrier(key_sums.astype(jnp.bfloat16))
        value_low = lax.optimization_barrier(value_sums.astype(jnp.bfloat16))
        terms = jnp.einsum('dtk,ctk->tdc', split_groups(key_rows, part_width), split_groups(key_low, part_width))
        terms = terms + jnp.einsum('dtk,ctk->tdc', split_groups(value_rows, part_width), split_groups(value_low, part_width))
        rounded = lax.optimization_barrier(terms.astype(jnp.bfloat16)).astype(jnp.float32)
        return lax.optimization_barrier(jnp.sum(rounded, axis=0))
    context = lax.optimization_barrier(jnp.sum(lax.map(context_step, (key_weight, value_weight, key_total, value_total)), axis=0))
    hidden_back = jnp.dot(text_weight, context.astype(jnp.bfloat16), preferred_element_type=jnp.float32)
    return (sent, hidden_back * gelu_slope(text_hidden.astype(jnp.float32)))
```

```python
import functools
import math

import jax
import jax.numpy as jnp
from jax import lax
from jax.experimental import pallas as pl
from jax.experimental.pallas import tpu as pltpu
from jax.sharding import PartitionSpec as P

HEAD = 128
NX, NZ = 4, 8
SECTIONS = NX * NZ
TENSOR = 4
VMEM_LIMIT = 40 * 1024 * 1024
F32 = jnp.float32
BF16 = jnp.bfloat16
NT = (((1,), (1,)), ((), ()))
NN = (((1,), (0,)), ((), ()))
TN = (((0,), (0,)), ((), ()))


def dot(a, b, dims):
    return lax.dot_general(a, b, dims, preferred_element_type=F32)


def positions():
    section = lax.axis_index("section")
    tensor = lax.axis_index("tensor")
    return jnp.stack(
        [
            section // NZ,
            section % NZ,
            tensor // 2,
            tensor % 2,
            (section == SECTIONS - 1).astype(jnp.int32),
        ]
    ).astype(jnp.int32)


def block_for(pos, j, other):
    core = pos[3] ^ other
    return (pos[2] ^ (j % 2)) * 2 + (core ^ (j // 2))


def swap_tensor(value, bit):
    return lax.ppermute(value, "tensor", [(i, i ^ bit) for i in range(TENSOR)])


def send_x(value, step):
    pairs = [
        (x * NZ + z, ((x + step) % NX) * NZ + z) for x in range(NX) for z in range(NZ)
    ]
    return lax.ppermute(value, "section", pairs)


def send_z(value, step):
    pairs = []
    for x in range(NX):
        for z in range(NZ):
            for t in range(TENSOR):
                to = (z + step + 4 * (t % 2)) % NZ
                pairs.append(((x * NZ + z) * TENSOR + t, (x * NZ + to) * TENSOR + t))
    return lax.ppermute(value, ("section", "tensor"), pairs)


def pass_back(value, bit):
    pairs = [
        ((s + 1) * TENSOR + t, s * TENSOR + (t ^ bit))
        for s in range(SECTIONS - 1)
        for t in range(TENSOR)
    ]
    return lax.ppermute(value, ("section", "tensor"), pairs)


def probabilities(q, k):
    factor = HEAD ** (-0.5) * math.log2(math.e)
    scores = dot(k, q, NT)
    peak = jnp.max(scores, axis=0, keepdims=True)
    shifted = jnp.exp2((scores - peak) * factor)
    return shifted * (1.0 / jnp.sum(shifted, axis=0, keepdims=True))


def score_gradient(attention, v, g):
    attention_grad = dot(v, g, NT)
    row_dot = jnp.sum(attention * attention_grad, axis=0, keepdims=True)
    return (attention * (attention_grad - row_dot)).astype(BF16)


def heads_of(width):
    return [slice(i, i + HEAD) for i in range(0, width, HEAD)]


def call(body, grid, in_specs, out_specs, out_shape, flops, nbytes, scratch=()):
    return pl.pallas_call(
        body,
        grid_spec=pltpu.PrefetchScalarGridSpec(
            num_scalar_prefetch=1,
            grid=grid,
            in_specs=in_specs,
            out_specs=out_specs,
            scratch_shapes=list(scratch),
        ),
        out_shape=out_shape,
        compiler_params=pltpu.CompilerParams(vmem_limit_bytes=VMEM_LIMIT),
        cost_estimate=pl.CostEstimate(flops=flops, bytes_accessed=nbytes, transcendentals=0),
    )


def full(*shape):
    return pl.BlockSpec(shape, lambda *a: (0,) * len(shape))


ANY = pl.BlockSpec(memory_space=pl.ANY)


def tick_spec(tick, rows, cols):
    return pl.BlockSpec((None, None, rows, cols), lambda *a: (0, tick, 0, 0))


def first_kernel(pos, q_ref, k_ref, v_ref, g_ref, w_ref, dq_ref, out_ref):
    @pl.when(pl.program_id(0) == 0)
    def _():
        for h in heads_of(q_ref.shape[-1]):
            k = k_ref[:, h]
            attention = probabilities(q_ref[:, h], k)
            score_grad = score_gradient(attention, v_ref[:, h], g_ref[:, h])
            dq = dot(score_grad, k, TN) * HEAD ** (-0.5)
            dq_ref[:, h] = dq.astype(BF16)

    out_ref[...] = dot(dq_ref[...], w_ref[...], NT).astype(BF16)


def project_kernel(pos, dq_ref, w_ref, out_ref):
    out_ref[...] = dot(dq_ref[...], w_ref[...], NT).astype(BF16)


def between_kernel(pos, q0_ref, q1_ref, k_ref, v_ref, g_ref, after, dk_ref, dv_ref, p_ref):
    for i, h in enumerate(heads_of(k_ref.shape[-1])):
        k = k_ref[:, h]
        q = q0_ref[:, h]
        g = g_ref[:, h]
        attention = probabilities(q, k)
        score_grad = score_gradient(attention, v_ref[:, h], g)
        dk_ref[:, h] = dot(score_grad, q, NN) * HEAD ** (-0.5)
        dv_ref[:, h] = dot(attention.astype(BF16), g, NN)
        p_ref[i] = probabilities(q1_ref[:, h], k)


def second_kernel(
    pos, q_ref, v_ref, a_ref, b_ref, top_ref, dk_ref, dv_ref, p_ref, g_ref, ds_ref, low_ref, held
):
    width = q_ref.shape[-1]
    came = a_ref[...].astype(F32) + b_ref[...].astype(F32)
    g_ref[...] = jnp.where(pos[4] == 1, top_ref[...].astype(F32), came).astype(BF16)
    for i, h in enumerate(heads_of(width)):
        g = g_ref[:, h]
        attention = p_ref[i]
        score_grad = score_gradient(attention, v_ref[:, h], g)
        ds_ref[i] = score_grad
        dk = dk_ref[:, h] + dot(score_grad, q_ref[:, h], NN) * HEAD ** (-0.5)
        dv = dv_ref[:, h] + dot(attention.astype(BF16), g, NN)
        held[:, h] = dk.astype(BF16)
        held[:, slice(width + h.start, width + h.stop)] = dv.astype(BF16)
    rows = held.shape[0] // SECTIONS
    for other in range(2):
        core = pos[3] ^ (1 - other)
        for dx in range(NX):
            for kz in range(NZ // 2):
                to_x = (pos[0] + dx) % NX
                to_z = (pos[1] + kz + 4 * core) % NZ
                source = pl.multiple_of((to_x * NZ + to_z) * rows, rows)
                place = ((other * NX + dx) * (NZ // 2) + kz) * rows
                low_ref[place : place + rows, :] = held[pl.ds(source, rows), :]


def context_kernel(pos, low_ref, kw_ref, vw_ref, *rest):
    out_ref = rest[-1]
    width = kw_ref.shape[-1]
    total = dot(low_ref[:, :width], kw_ref[...], NT) + dot(low_ref[:, width:], vw_ref[...], NT)
    out_ref[...] = total.astype(BF16)


def third_kernel(pos, ds_ref, k_ref, w_ref, after, dq_ref, out_ref):
    @pl.when(pl.program_id(0) == 0)
    def _():
        for i, h in enumerate(heads_of(k_ref.shape[-1])):
            dq = dot(ds_ref[i], k_ref[:, h], TN) * HEAD ** (-0.5)
            dq_ref[:, h] = dq.astype(BF16)

    out_ref[...] = dot(dq_ref[...], w_ref[...], NT).astype(BF16)


def text_kernel(pos, context_ref, w_ref, out_ref):
    out_ref[...] = dot(context_ref[...], w_ref[...], NT).astype(BF16)


def sent_kernel(pos, a0_ref, b0_ref, a1_ref, b1_ref, out_ref):
    out_ref[0] = (a0_ref[...].astype(F32) + b0_ref[...].astype(F32)).astype(BF16)
    out_ref[1] = (a1_ref[...].astype(F32) + b1_ref[...].astype(F32)).astype(BF16)


def smooth_gate(inputs):
    return jax.nn.gelu(inputs, approximate=True)


def gelu_slope(inputs):
    unused_out, backward = jax.vjp(smooth_gate, inputs)
    return backward(jnp.ones_like(inputs))[0]


def add_low(*terms):
    total = terms[0].astype(F32)
    for term in terms[1:]:
        total = total + term.astype(F32)
    return total.astype(BF16)


def shards(
    grad_in,
    grad_top,
    queries,
    keys,
    values,
    query_weight,
    key_weight,
    value_weight,
    text_weight,
    text_hidden,
):
    pos = positions()
    rows, width = grad_in.shape[1], grad_in.shape[2]
    text = keys.shape[1]
    heads = width // HEAD
    model = width * TENSOR
    k, v, g0, top = keys[0], values[0], grad_in[0], grad_top[0]
    wq, wk, wv = query_weight[0], key_weight[0], value_weight[0]

    z_groups = [[x * NZ + z for z in range(NZ)] for x in range(NX)]
    x_groups = [[x * NZ + z for x in range(NX)] for z in range(NZ)]
    gathered = lax.all_gather(
        text_weight, "section", axis=0, tiled=True, axis_index_groups=z_groups
    )
    gathered = lax.all_gather(gathered, "section", axis=0, tiled=True, axis_index_groups=x_groups)

    act = jax.ShapeDtypeStruct((rows, width), BF16)
    pair = jax.ShapeDtypeStruct((2, rows, width), BF16)
    pair_spec = pl.BlockSpec((None, rows, width), lambda j, pos: (j, 0, 0))

    def weight_spec(other):
        return pl.BlockSpec((width, width), lambda j, pos: (block_for(pos, j, other), 0))

    project_flops = 4 * rows * width * width
    head_flops = 2 * rows * text * width

    dq0, send0 = call(
        first_kernel,
        (2,),
        [
            tick_spec(0, rows, width),
            full(text, width),
            full(text, width),
            full(rows, width),
            weight_spec(1),
        ],
        [full(rows, width), pair_spec],
        [act, pair],
        project_flops + 3 * head_flops,
        8_000_000,
    )(pos, queries, k, v, g0, wq)
    came0 = swap_tensor(send0, 1)
    keep0 = call(
        project_kernel,
        (2,),
        [full(rows, width), weight_spec(0)],
        pair_spec,
        pair,
        project_flops,
        2_600_000,
    )(pos, dq0, wq)
    near0 = add_low(g0, keep0[0], came0[0])
    far0 = add_low(keep0[1], came0[1])
    from_near = pass_back(near0, 0)
    from_far = pass_back(far0, 2)

    square = jax.ShapeDtypeStruct((text, width), F32)
    dk0, dv0, p1 = call(
        between_kernel,
        (1,),
        [
            tick_spec(0, rows, width),
            tick_spec(1, rows, width),
            full(text, width),
            full(text, width),
            full(rows, width),
            ANY,
        ],
        [full(text, width), full(text, width), full(heads, text, rows)],
        [square, square, jax.ShapeDtypeStruct((heads, text, rows), F32)],
        6 * head_flops,
        8_000_000,
    )(pos, queries, queries, k, v, g0, far0)

    g1, ds1, low = call(
        second_kernel,
        (1,),
        [
            tick_spec(1, rows, width),
            full(text, width),
            full(rows, width),
            full(rows, width),
            full(rows, width),
            full(text, width),
            full(text, width),
            full(heads, text, rows),
        ],
        [full(rows, width), full(heads, text, rows), full(text, 2 * width)],
        [
            act,
            jax.ShapeDtypeStruct((heads, text, rows), BF16),
            jax.ShapeDtypeStruct((text, 2 * width), BF16),
        ],
        3 * head_flops,
        10_000_000,
        [pltpu.VMEM((text, 2 * width), BF16)],
    )(pos, queries, v, from_near, from_far, top, dk0, dv0, p1)
    far0_back = swap_tensor(far0, 2)

    def context_half(other, *after):
        weight = pl.BlockSpec((width, width), lambda j, pos: (block_for(pos, j, other), 0))
        return call(
            context_kernel,
            (TENSOR,),
            [pl.BlockSpec((text // 2, 2 * width), lambda j, pos: (1 - other, 0)), weight, weight]
            + [ANY] * len(after),
            pl.BlockSpec((text // 2, width), lambda j, pos: (0, j)),
            jax.ShapeDtypeStruct((text // 2, model), BF16),
            2 * text * width * model,
            8_000_000,
        )(pos, low, wk, wv, *after)

    send = context_half(1)
    keep = context_half(0, send)
    came = swap_tensor(send, 1)
    part = text // 2 // NX
    by_x = [
        add_low(keep[i * part : (i + 1) * part], came[i * part : (i + 1) * part])
        for i in range(NX)
    ]
    came_x = [send_x(by_x[i], i) for i in range(1, NX)]

    dq1, send1 = call(
        third_kernel,
        (2,),
        [full(heads, text, rows), full(text, width), weight_spec(1), ANY],
        [full(rows, width), pair_spec],
        [act, pair],
        project_flops + head_flops,
        5_000_000,
    )(pos, ds1, k, wq, by_x[1])
    came1 = swap_tensor(send1, 1)
    keep1 = call(
        project_kernel,
        (2,),
        [full(rows, width), weight_spec(0)],
        pair_spec,
        pair,
        project_flops,
        2_600_000,
    )(pos, dq1, wq)
    near1 = add_low(g1, keep1[0], came1[0])
    far1 = add_low(keep1[1], came1[1])
    far1_back = swap_tensor(far1, 2)
    sent = call(
        sent_kernel,
        (1,),
        [full(rows, width)] * 4,
        full(2, rows, width),
        jax.ShapeDtypeStruct((2, rows, width), BF16),
        1_000_000,
        2_000_000,
    )(pos, near0, far0_back, near1, far1_back)

    by_z = add_low(by_x[0], *came_x)
    few = part // (NZ // 2)
    came_z = [send_z(by_z[i * few : (i + 1) * few], i) for i in range(NZ // 2)]

    def over_tensor(terms):
        total = sum(term.astype(F32) for term in terms)
        half = total.shape[1] // 2
        came = swap_tensor(total[:, half:].astype(BF16), 1)
        total = total[:, :half] + came.astype(F32)
        half = total.shape[1] // 2
        came = swap_tensor(total[:, half:].astype(BF16), 2)
        return total[:, :half] + came.astype(F32)

    context = over_tensor(came_z).astype(BF16)
    hidden = call(
        text_kernel,
        (TENSOR,),
        [
            full(few, width),
            pl.BlockSpec((width, width), lambda j, pos: (block_for(pos, j, 0), 0)),
        ],
        pl.BlockSpec((few, width), lambda j, pos: (0, j)),
        jax.ShapeDtypeStruct((few, model), BF16),
        2 * few * width * model,
        3_300_000,
    )(pos, context, gathered)
    hidden_back = over_tensor([hidden])
    text_grad = hidden_back.T * gelu_slope(text_hidden.astype(F32))
    return (sent[None], text_grad)


def solution(mesh):
    placed = (
        P("section", "dp", "tensor"),
        P(None, "dp", "tensor"),
        P("section", None, "dp", "tensor"),
        P("section", "dp", "tensor"),
        P("section", "dp", "tensor"),
        P("section", None, "tensor"),
        P("section", None, "tensor"),
        P("section", None, "tensor"),
        P("section", "tensor"),
        P("tensor", ("dp", "section")),
    )
    return jax.shard_map(
        shards,
        mesh=mesh,
        in_specs=placed,
        out_specs=(P("section", None, "dp", "tensor"), P("tensor", ("dp", "section"))),
        check_vma=False,
    )
```

```python
import functools
import math

import jax
import jax.numpy as jnp
from jax import lax
from jax.experimental import pallas as pl
from jax.experimental.pallas import tpu as pltpu
from jax.sharding import PartitionSpec as P

HEAD = 128
NX, NZ = 4, 8
SECTIONS = NX * NZ
TENSOR = 4
VMEM_LIMIT = 20 * 1024 * 1024
F32 = jnp.float32
BF16 = jnp.bfloat16
NT = (((1,), (1,)), ((), ()))
NN = (((1,), (0,)), ((), ()))
TN = (((0,), (0,)), ((), ()))


def dot(a, b, dims):
    return lax.dot_general(a, b, dims, preferred_element_type=F32)


def positions():
    section = lax.axis_index("section")
    tensor = lax.axis_index("tensor")
    return jnp.stack(
        [
            section // NZ,
            section % NZ,
            tensor // 2,
            tensor % 2,
            (section == SECTIONS - 1).astype(jnp.int32),
        ]
    ).astype(jnp.int32)


def block_for(pos, j, other):
    core = pos[3] ^ other
    return (pos[2] ^ (j % 2)) * 2 + (core ^ (j // 2))


def swap_tensor(value, bit):
    return lax.ppermute(value, "tensor", [(i, i ^ bit) for i in range(TENSOR)])


def send_x(value, step):
    pairs = [
        (x * NZ + z, ((x + step) % NX) * NZ + z) for x in range(NX) for z in range(NZ)
    ]
    return lax.ppermute(value, "section", pairs)


def send_z(value, step):
    pairs = []
    for x in range(NX):
        for z in range(NZ):
            for t in range(TENSOR):
                to = (z + step + 4 * (t % 2)) % NZ
                pairs.append(((x * NZ + z) * TENSOR + t, (x * NZ + to) * TENSOR + t))
    return lax.ppermute(value, ("section", "tensor"), pairs)


def turn(value, bits):
    pairs = [
        ((x * NZ + z) * TENSOR + t, (t * NZ + (z ^ bits)) * TENSOR + x)
        for x in range(NX)
        for z in range(NZ)
        for t in range(TENSOR)
    ]
    return lax.ppermute(value, ("section", "tensor"), pairs)


def swap_z(value, bits):
    pairs = [(s, s // NZ * NZ + ((s % NZ) ^ bits)) for s in range(SECTIONS)]
    return lax.ppermute(value, "section", pairs)


def from_z(value, step):
    pairs = [(s, s // NZ * NZ + (s - step) % NZ) for s in range(SECTIONS)]
    return lax.ppermute(value, "section", pairs)


def pass_back(value):
    return lax.ppermute(value, "section", [(s + 1, s) for s in range(SECTIONS - 1)])


def weights_of(q, k):
    factor = HEAD ** (-0.5) * math.log2(math.e)
    scores = dot(k, q, NT)
    peak = jnp.max(scores, axis=0, keepdims=True)
    shifted = jnp.exp2((scores - peak) * factor)
    return shifted, 1.0 / jnp.sum(shifted, axis=0, keepdims=True)


def score_gradient(shifted, factor, v, g):
    attention_grad = dot(v, g, NT)
    row_dot = jnp.sum(shifted * attention_grad, axis=0, keepdims=True) * factor
    return (shifted * (attention_grad * factor - row_dot * factor)).astype(BF16)


def heads_of(width):
    return [slice(i, i + HEAD) for i in range(0, width, HEAD)]

HBM = pl.BlockSpec(memory_space=pltpu.HBM)
VMEM = pl.BlockSpec(memory_space=pltpu.VMEM)
ANY = pl.BlockSpec(memory_space=pl.ANY)


def call(body, ins, outs, scratch=(), place=VMEM):
    arrays = [
        pltpu.with_memory_space_constraint(array, pltpu.HBM) if spec is HBM else array
        for array, spec in ins
    ]
    shapes = [jax.ShapeDtypeStruct(*out) for out in outs]
    return pl.pallas_call(
        body,
        in_specs=[spec for array, spec in ins],
        out_specs=[place] * len(shapes),
        out_shape=shapes,
        scratch_shapes=list(scratch),
        compiler_params=pltpu.CompilerParams(vmem_limit_bytes=VMEM_LIMIT),
        cost_estimate=pl.CostEstimate(flops=1, bytes_accessed=1, transcendentals=0),
    )(*arrays)


def copies(pairs, sems):
    started = []
    for i, (source, target) in enumerate(pairs):
        started.append(pltpu.make_async_copy(source, target, sems.at[i]))
        started[-1].start()
    return started


def rows_of(ref, block, count):
    return ref[pl.ds(pl.multiple_of(block * count, count), count), :]


def first_kernel(
    pos, q_hbm, k_hbm, v_hbm, g_hbm, w_hbm, dq_ref, w_ref, g_ref, q_ref, k_ref, v_ref, sems
):
    width = k_ref.shape[-1]
    heads = heads_of(width)
    pairs = []
    for h in heads:
        pairs.append((k_hbm.at[0, :, h], k_ref.at[:, h]))
        pairs.append((q_hbm.at[0, 0, :, h], q_ref.at[:, h]))
        pairs.append((v_hbm.at[0, :, h], v_ref.at[:, h]))
        pairs.append((g_hbm.at[0, :, h], g_ref.at[:, h]))
    pairs.append((w_hbm.at[0], w_ref))
    started = copies(pairs, sems)
    for i, h in enumerate(heads):
        for copy in started[4 * i : 4 * i + 4]:
            copy.wait()
        k = k_ref[:, h]
        shifted, factor = weights_of(q_ref[:, h], k)
        score_grad = score_gradient(shifted, factor, v_ref[:, h], g_ref[:, h])
        dq_ref[:, h] = (dot(score_grad, k, TN) * HEAD ** (-0.5)).astype(BF16)
    started[-1].wait()


def project_kernel(other, pos, dq_ref, w_ref, *rest):
    out_ref = rest[-1]
    width = w_ref.shape[-1]
    for j in range(2):
        weight = rows_of(w_ref, block_for(pos, j, other), width)
        out_ref[j] = dot(dq_ref[...], weight, NT).astype(BF16)


def meet_core_kernel(pos, g_ref, keep_ref, came_ref, near_ref, far_ref):
    near = keep_ref[0].astype(F32) + came_ref[0].astype(F32)
    near_ref[...] = near + g_ref[...].astype(F32)
    far_ref[...] = (keep_ref[1].astype(F32) + came_ref[1].astype(F32)).astype(BF16)


def meet_far_kernel(pos, near_ref, far_ref, text_a, text_b, after, out_ref, text_ref):
    out_ref[...] = (near_ref[...] + far_ref[...].astype(F32)).astype(BF16)
    text_ref[0] = text_a[...]
    text_ref[1] = text_b[...]


def between_kernel(
    pos,
    q_hbm,
    k_hbm,
    v_hbm,
    g_hbm,
    top_hbm,
    wk_hbm,
    wv_hbm,
    after,
    dk_ref,
    dv_ref,
    q_ref,
    k_ref,
    v_ref,
    top_ref,
    wk_ref,
    wv_ref,
    q0_ref,
    g_ref,
    sems,
):
    pairs = [(q_hbm.at[0, 0], q0_ref), (g_hbm.at[0], g_ref)]
    rows = k_ref.shape[0] // SECTIONS
    for other in range(2):
        core = pos[3] ^ (1 - other)
        for kz in range(NZ // 2):
            to_z = (pos[1] + kz + 4 * core) % NZ
            for to_x in range(NX):
                source = pl.ds(pl.multiple_of((to_x * NZ + to_z) * rows, rows), rows)
                place = pl.ds(((other * (NZ // 2) + kz) * NX + to_x) * rows, rows)
                pairs.append((k_hbm.at[0, source], k_ref.at[place]))
                pairs.append((v_hbm.at[0, source], v_ref.at[place]))
    first = len(pairs)
    pairs.append((q_hbm.at[0, 1], q_ref))
    pairs.append((top_hbm.at[0], top_ref))
    pairs.append((wk_hbm.at[0], wk_ref))
    pairs.append((wv_hbm.at[0], wv_ref))
    started = copies(pairs, sems)
    for copy in started[:first]:
        copy.wait()
    for h in heads_of(k_ref.shape[-1]):
        q = q0_ref[:, h]
        g = g_ref[:, h]
        shifted, factor = weights_of(q, k_ref[:, h])
        score_grad = score_gradient(shifted, factor, v_ref[:, h], g)
        dk_ref[:, h] = dot(score_grad, q, NN) * HEAD ** (-0.5)
        dv_ref[:, h] = dot((shifted * factor).astype(BF16), g, NN)
    for copy in started[first:]:
        copy.wait()


def ahead_kernel(pos, q_ref, k_ref, after, p_ref, low_ref):
    for i, h in enumerate(heads_of(k_ref.shape[-1])):
        shifted, factor = weights_of(q_ref[:, h], k_ref[:, h])
        attention = shifted * factor
        p_ref[i] = attention
        low_ref[i] = attention.astype(BF16)


def second_kernel(
    pos, q_ref, v_ref, came_ref, top_ref, dk_ref, dv_ref, p_ref, p_low_ref, g_ref, ds_ref, low_ref
):
    width = q_ref.shape[-1]
    g_ref[...] = jnp.where(pos[4] == 1, top_ref[...].astype(F32), came_ref[...].astype(F32)).astype(
        BF16
    )
    for i, h in enumerate(heads_of(width)):
        g = g_ref[:, h]
        attention_grad = dot(v_ref[:, h], g, NT)
        row_dot = jnp.sum(p_ref[i] * attention_grad, axis=0, keepdims=True)
        score_grad = (p_ref[i] * (attention_grad - row_dot)).astype(BF16)
        ds_ref[i] = score_grad
        dk = dk_ref[:, h] + dot(score_grad, q_ref[:, h], NN) * HEAD ** (-0.5)
        dv = dv_ref[:, h] + dot(p_low_ref[i], g, NN)
        low_ref[:, h] = dk.astype(BF16)
        low_ref[:, slice(width + h.start, width + h.stop)] = dv.astype(BF16)


def context_block(pos, step, half, low_ref, kw_ref, vw_ref):
    width = kw_ref.shape[-1]
    count = low_ref.shape[0] // 2
    rows = slice(half * count, (half + 1) * count)
    block = (pos[0] + step) % NX
    total = dot(rows_of(kw_ref, block, width), low_ref[rows, :width], NT)
    return total + dot(rows_of(vw_ref, block, width), low_ref[rows, width:], NT)


def context_kernel(half, pos, low_ref, kw_ref, vw_ref, *rest):
    out_ref = rest[-1]
    for step in range(NX):
        total = context_block(pos, step, half, low_ref, kw_ref, vw_ref)
        out_ref[step] = total.astype(BF16)


def x_add_kernel(pos, keep_ref, came_ref, two_ref, late_two, *outs):
    late_two[...] = two_ref[...]
    for i, out in enumerate(outs):
        out[...] = (keep_ref[i + 1].astype(F32) + came_ref[i + 1].astype(F32)).astype(BF16)


def z_add_kernel(pos, keep_ref, came_ref, b_ref, c_ref, d_ref, *outs):
    rows = outs[0].shape[0]
    width = outs[0].shape[1]
    for place in (slice(0, width // 2), slice(width // 2, width)):
        total = keep_ref[0, place, :].astype(F32) + came_ref[0, place, :].astype(F32)
        total = total + b_ref[place, :].astype(F32)
        total = total + c_ref[place, :].astype(F32) + d_ref[place, :].astype(F32)
        total = total.T.astype(BF16)
        for j, out in enumerate(outs):
            out[:, place] = total[j * rows : (j + 1) * rows]


def third_kernel(
    pos,
    ds_ref,
    k_ref,
    w_ref,
    g_ref,
    after,
    near_ref,
    far_out,
    core_out,
    both_out,
    dq_ref,
):
    width = w_ref.shape[-1]
    for i, h in enumerate(heads_of(width)):
        dq_ref[:, h] = (dot(ds_ref[i], k_ref[:, h], TN) * HEAD ** (-0.5)).astype(BF16)
    for j, out in enumerate((near_ref, far_out, core_out, both_out)):
        weight = rows_of(w_ref, block_for(pos, j, 0), width)
        total = dot(dq_ref[...], weight, NT)
        if j == 0:
            total = total + g_ref[...].astype(F32)
        out[...] = total.astype(out.dtype)


def z_sum_kernel(pos, a_ref, b_ref, c_ref, d_ref, after, keep_ref, send_ref):
    total = a_ref[...].astype(F32) + b_ref[...].astype(F32)
    total = total + c_ref[...].astype(F32) + d_ref[...].astype(F32)
    keep_ref[...] = total
    send_ref[...] = total.astype(BF16)


def core_sum_kernel(pos, keep_ref, came_ref, out_ref, send_ref):
    total = keep_ref[...] + came_ref[...].astype(F32)
    out_ref[...] = total
    send_ref[...] = total.astype(BF16)


def text_kernel(pos, keep_ref, far_ref, own, two, up, down, *rest):
    *outs, context_ref, w_ref = rest
    rows = own.shape[1]
    places = (pos[1], pos[1] ^ 2, (pos[1] + 1) % NZ, (pos[1] + NZ - 1) % NZ)
    for ref, z in zip((own, two, up, down), places):
        for r in range(2):
            row = pl.multiple_of((z ^ (4 * r)) * rows, rows)
            w_ref[pl.ds(row, rows), :] = ref[r]
    context_ref[...] = (keep_ref[...] + far_ref[...].astype(F32)).astype(BF16)
    tokens = outs[0].shape[0]
    for i, out in enumerate(outs):
        row = pl.multiple_of((pos[0] + i) % NX * tokens, tokens)
        total = dot(context_ref[pl.ds(row, tokens), :], w_ref[...], NT)
        out[...] = total.astype(out.dtype)


def sent_kernel(pos, first_ref, a_ref, b_ref, c_ref, d_ref, out_hbm, out_ref, sems):
    out_ref[0] = first_ref[...]
    total = a_ref[...] + b_ref[...].astype(F32)
    total = total + c_ref[...].astype(F32) + d_ref[...].astype(F32)
    out_ref[1] = total.astype(BF16)
    copies([(out_ref, out_hbm)], sems)[0].wait()


def smooth_gate(inputs):
    return jax.nn.gelu(inputs, approximate=True)


def gelu_slope(inputs):
    unused_out, backward = jax.vjp(smooth_gate, inputs)
    return backward(jnp.ones_like(inputs))[0]


def shards(
    grad_in,
    grad_top,
    queries,
    keys,
    values,
    query_weight,
    key_weight,
    value_weight,
    text_weight,
    text_hidden,
):
    pos = positions()
    rows, width = grad_in.shape[1], grad_in.shape[2]
    text = keys.shape[1]
    heads = width // HEAD
    model = width * TENSOR
    where = (pos, pl.BlockSpec(memory_space=pltpu.SMEM))

    act = ((rows, width), BF16)
    pair = ((2, rows, width), BF16)
    square = ((text, width), F32)
    narrow = ((text, width), BF16)
    matrix = ((model, width), BF16)

    def vm(*shape_dtype):
        return pltpu.VMEM(*shape_dtype)

    def dma(count):
        return pltpu.SemaphoreType.DMA((count,))

    block = text_weight.shape
    text_a, text_b = turn(text_weight, 0), turn(text_weight, 4)

    dq0, wq, g_first = call(
        first_kernel,
        [where, (queries, HBM), (keys, HBM), (values, HBM), (grad_in, HBM), (query_weight, HBM)],
        [act, matrix, act],
        [vm(*act), vm(*narrow), vm(*narrow), dma(4 * heads + 1)],
    )
    def project(other, *after):
        return call(
            functools.partial(project_kernel, other),
            [where, (dq0, VMEM), (wq, VMEM)] + [(a, ANY) for a in after],
            [pair],
        )[0]

    send0 = project(1)
    came0 = swap_tensor(send0, 1)
    keep0 = project(0, send0)
    near0, far0 = call(
        meet_core_kernel,
        [where] + [(a, VMEM) for a in (g_first, keep0, came0)],
        [((rows, width), F32), act],
    )
    far0_back = swap_tensor(far0, 2)

    dk0, dv0, q1, k, v, top, wk, wv = call(
        between_kernel,
        [
            where,
            (queries, HBM),
            (keys, HBM),
            (values, HBM),
            (grad_in, HBM),
            (grad_top, HBM),
            (key_weight, HBM),
            (value_weight, HBM),
            (far0, ANY),
        ],
        [square, square, act, narrow, narrow, act, matrix, matrix],
        [vm(*act), vm(*act), dma(2 * SECTIONS + 6)],
    )

    sent0, text_two = call(
        meet_far_kernel,
        [where] + [(a, VMEM) for a in (near0, far0_back, text_a, text_b)]
        + [(dk0, ANY)],
        [act, ((2,) + block, BF16)],
    )
    came_back = pass_back(sent0)
    p1, p1_low = call(
        ahead_kernel,
        [where, (q1, VMEM), (k, VMEM), (sent0, ANY)],
        [((heads, text, rows), F32), ((heads, text, rows), BF16)],
    )

    g1, ds1, low = call(
        second_kernel,
        [where] + [(a, VMEM) for a in (q1, v, came_back, top, dk0, dv0, p1, p1_low)],
        [act, ((heads, text, rows), BF16), ((text, 2 * width), BF16)],
    )

    terms = ((NX, width, text // 2), BF16)
    (send,) = call(
        functools.partial(context_kernel, 0), [where, (low, VMEM), (wk, VMEM), (wv, VMEM)], [terms]
    )
    came = swap_tensor(send, 1)
    (keep,) = call(
        functools.partial(context_kernel, 1),
        [where, (low, VMEM), (wk, VMEM), (wv, VMEM), (send, ANY)],
        [terms],
    )
    text_two, *by_x = call(
        x_add_kernel,
        [where, (keep, VMEM), (came, VMEM), (text_two, VMEM)],
        [((2,) + block, BF16)] + [((width, text // 2), BF16)] * (NX - 1),
    )
    came_x = [send_x(piece, i + 1) for i, piece in enumerate(by_x)]
    text_more = [swap_z(text_two, 2), from_z(text_two, 1), from_z(text_two, -1)]

    near1, far1, core1, both1 = call(
        third_kernel,
        [where, (ds1, VMEM), (k, VMEM), (wq, VMEM), (g1, VMEM), (by_x[1], ANY)],
        [((rows, width), F32)] + [act] * 3,
        [vm(*act)],
    )
    others = (
        near1,
        swap_tensor(far1, 2),
        swap_tensor(core1, 1),
        swap_tensor(both1, 3),
    )
    (sent,) = call(
        sent_kernel,
        [where, (sent0, VMEM)] + [(a, VMEM) for a in others],
        [pair],
        [vm(*pair), dma(1)],
        ANY,
    )

    few = text // NZ
    by_z = call(
        z_add_kernel,
        [where] + [(a, VMEM) for a in (keep, came, *came_x)],
        [((few, width), BF16)] * (NZ // 2),
    )
    came_z = [send_z(by_z[i], i) for i in range(NZ // 2)]
    context, context_low = call(
        z_sum_kernel,
        [where] + [(a, VMEM) for a in came_z] + [(sent, HBM)],
        [((few, width), F32), ((few, width), BF16)],
    )
    context, context_low = call(
        core_sum_kernel,
        [where, (context, VMEM), (swap_tensor(context_low, 1), VMEM)],
        [((few, width), F32), ((few, width), BF16)],
    )
    far_context = swap_tensor(context_low, 2)
    tokens = few // NX
    hidden, *to_send = call(
        text_kernel,
        [where] + [(a, VMEM) for a in (context, far_context, text_two, *text_more)],
        [((tokens, width), F32)] + [((tokens, width), BF16)] * (NX - 1),
        [vm((few, width), BF16), vm((width, width), BF16)],
    )
    for i, piece in enumerate(to_send):
        hidden = hidden + send_x(piece, i + 1).astype(F32)
    text_grad = hidden.T * gelu_slope(text_hidden.astype(F32))
    return (sent[None], text_grad)


def solution(mesh):
    placed = (
        P("section", "dp", "tensor"),
        P(None, "dp", "tensor"),
        P("section", None, "dp", "tensor"),
        P("section", "dp", "tensor"),
        P("section", "dp", "tensor"),
        P("section", None, "tensor"),
        P("section", None, "tensor"),
        P("section", None, "tensor"),
        P("section", "tensor"),
        P("tensor", ("dp", "section")),
    )
    return jax.shard_map(
        shards,
        mesh=mesh,
        in_specs=placed,
        out_specs=(P("section", None, "dp", "tensor"), P("tensor", ("dp", "section"))),
        check_vma=False,
    )
```

```python
import functools
import math

import jax
import jax.numpy as jnp
from jax import lax
from jax.experimental import pallas as pl
from jax.experimental.pallas import tpu as pltpu
from jax.sharding import PartitionSpec as P

HEAD = 128
NX, NZ = 4, 8
SECTIONS = NX * NZ
TENSOR = 4
LONG = 40_000_000_000
VMEM_LIMIT = 20 * 1024 * 1024
F32 = jnp.float32
BF16 = jnp.bfloat16
NT = (((1,), (1,)), ((), ()))
NN = (((1,), (0,)), ((), ()))
TN = (((0,), (0,)), ((), ()))


def dot(a, b, dims):
    return lax.dot_general(a, b, dims, preferred_element_type=F32)


def positions():
    section = lax.axis_index("section")
    tensor = lax.axis_index("tensor")
    return jnp.stack(
        [
            section // NZ,
            section % NZ,
            tensor // 2,
            tensor % 2,
            (section == SECTIONS - 1).astype(jnp.int32),
        ]
    ).astype(jnp.int32)


def block_for(pos, j, other):
    core = pos[3] ^ other
    return (pos[2] ^ (j % 2)) * 2 + (core ^ (j // 2))


def swap_tensor(value, bit):
    return lax.ppermute(value, "tensor", [(i, i ^ bit) for i in range(TENSOR)])


def send_x(value, step):
    pairs = [
        (x * NZ + z, ((x + step) % NX) * NZ + z) for x in range(NX) for z in range(NZ)
    ]
    return lax.ppermute(value, "section", pairs)


def send_z(value, step):
    pairs = []
    for x in range(NX):
        for z in range(NZ):
            for t in range(TENSOR):
                to = (z + step + 4 * (t % 2)) % NZ
                pairs.append(((x * NZ + z) * TENSOR + t, (x * NZ + to) * TENSOR + t))
    return lax.ppermute(value, ("section", "tensor"), pairs)


def turn(value):
    pairs = [
        ((x * NZ + z) * TENSOR + t, (t * NZ + z) * TENSOR + x)
        for x in range(NX)
        for z in range(NZ)
        for t in range(TENSOR)
    ]
    return lax.ppermute(value, ("section", "tensor"), pairs)


def swap_z(value, bits):
    pairs = [(s, s // NZ * NZ + ((s % NZ) ^ bits)) for s in range(SECTIONS)]
    return lax.ppermute(value, "section", pairs)


def from_z(value, step):
    pairs = [(s, s // NZ * NZ + (s - step) % NZ) for s in range(SECTIONS)]
    return lax.ppermute(value, "section", pairs)


def pass_back(value):
    return lax.ppermute(value, "section", [(s + 1, s) for s in range(SECTIONS - 1)])


def weights_of(q, k):
    factor = HEAD ** (-0.5) * math.log2(math.e)
    scores = dot(k, q, NT)
    peak = jnp.max(scores, axis=0, keepdims=True)
    shifted = jnp.exp2((scores - peak) * factor)
    return shifted, 1.0 / jnp.sum(shifted, axis=0, keepdims=True)


def score_gradient(shifted, factor, v, g):
    attention_grad = dot(v, g, NT)
    row_dot = jnp.sum(shifted * attention_grad, axis=0, keepdims=True) * factor
    return (shifted * (attention_grad * factor - row_dot * factor)).astype(BF16)


def heads_of(width):
    return [slice(i, i + HEAD) for i in range(0, width, HEAD)]

HBM = pl.BlockSpec(memory_space=pltpu.HBM)
VMEM = pl.BlockSpec(memory_space=pltpu.VMEM)
ANY = pl.BlockSpec(memory_space=pl.ANY)


def call(body, ins, outs, scratch=(), place=VMEM, flops=1):
    arrays = [
        pltpu.with_memory_space_constraint(array, pltpu.HBM) if spec is HBM else array
        for array, spec in ins
    ]
    shapes = [jax.ShapeDtypeStruct(*out) for out in outs]
    return pl.pallas_call(
        body,
        in_specs=[spec for array, spec in ins],
        out_specs=[place] * len(shapes),
        out_shape=shapes,
        scratch_shapes=list(scratch),
        compiler_params=pltpu.CompilerParams(vmem_limit_bytes=VMEM_LIMIT),
        cost_estimate=pl.CostEstimate(flops=flops, bytes_accessed=1, transcendentals=0),
    )(*arrays)


def copies(pairs, sems):
    started = []
    for i, (source, target) in enumerate(pairs):
        started.append(pltpu.make_async_copy(source, target, sems.at[i]))
        started[-1].start()
    return started


def rows_of(ref, block, count):
    return ref[pl.ds(pl.multiple_of(block * count, count), count), :]


def first_kernel(
    pos, q_hbm, k_hbm, v_hbm, g_hbm, w_hbm, dq_ref, w_ref, g_ref, q_ref, k_ref, v_ref, sems
):
    width = k_ref.shape[-1]
    heads = heads_of(width)
    refs = ((k_hbm.at[0], k_ref), (q_hbm.at[0, 0], q_ref), (v_hbm.at[0], v_ref), (g_hbm.at[0], g_ref))
    parts = (slice(0, HEAD), slice(HEAD, width))
    pairs = [(source.at[:, part], target.at[:, part]) for part in parts for source, target in refs]
    pairs.append((w_hbm.at[0], w_ref))
    started = copies(pairs, sems)
    for i, h in enumerate(heads):
        for copy in started[4 * i : 4 * i + 4] if i < 2 else ():
            copy.wait()
        k = k_ref[:, h]
        shifted, factor = weights_of(q_ref[:, h], k)
        score_grad = score_gradient(shifted, factor, v_ref[:, h], g_ref[:, h])
        dq_ref[h, :] = (dot(k, score_grad, TN) * HEAD ** (-0.5)).astype(BF16)
    started[-1].wait()


def project_kernel(other, pos, dq_ref, w_ref, *rest):
    out_ref = rest[-1]
    width = w_ref.shape[-1]
    for j in range(2):
        weight = rows_of(w_ref, block_for(pos, j, other), width)
        out_ref[j] = dot(weight, dq_ref[...], NN).astype(BF16)


def meet_core_kernel(pos, keep_ref, came_ref, near_ref, far_ref):
    near_ref[...] = keep_ref[0].astype(F32) + came_ref[0].astype(F32)
    far_ref[...] = (keep_ref[1].astype(F32) + came_ref[1].astype(F32)).astype(BF16)


def meet_far_kernel(pos, g_ref, near_ref, far_ref, text, after, out_ref, text_ref):
    text_ref[...] = text[...]
    total = (near_ref[...] + far_ref[...].astype(F32)).T
    out_ref[...] = (total + g_ref[...].astype(F32)).astype(BF16)


def between_kernel(
    pos,
    q_hbm,
    k_hbm,
    v_hbm,
    g_hbm,
    top_hbm,
    wk_hbm,
    wv_hbm,
    after,
    dk_ref,
    dv_ref,
    q_ref,
    k_ref,
    v_ref,
    top_ref,
    wkv_ref,
    q0_ref,
    g_ref,
    sems,
):
    pairs = [(q_hbm.at[0, 0], q0_ref), (g_hbm.at[0], g_ref)]
    rows = k_ref.shape[0] // SECTIONS
    for other in range(2):
        core = pos[3] ^ (1 - other)
        for kz in range(NZ // 2):
            to_z = (pos[1] + kz + 4 * core) % NZ
            for to_x in range(NX):
                source = pl.ds(pl.multiple_of((to_x * NZ + to_z) * rows, rows), rows)
                place = pl.ds(((other * (NZ // 2) + kz) * NX + to_x) * rows, rows)
                pairs.append((k_hbm.at[0, source], k_ref.at[place]))
                pairs.append((v_hbm.at[0, source], v_ref.at[place]))
    first = len(pairs)
    pairs.append((q_hbm.at[0, 1], q_ref))
    pairs.append((top_hbm.at[0], top_ref))
    width = k_ref.shape[-1]
    pairs.append((wk_hbm.at[0], wkv_ref.at[:, :width]))
    pairs.append((wv_hbm.at[0], wkv_ref.at[:, width:]))
    started = copies(pairs, sems)
    for copy in started[:first]:
        copy.wait()
    for h in heads_of(k_ref.shape[-1]):
        q = q0_ref[:, h]
        g = g_ref[:, h]
        shifted, factor = weights_of(q, k_ref[:, h])
        score_grad = score_gradient(shifted, factor, v_ref[:, h], g)
        dk_ref[:, h] = dot(score_grad, q, NN) * HEAD ** (-0.5)
        dv_ref[:, h] = dot((shifted * factor).astype(BF16), g, NN)
    for copy in started[first:]:
        copy.wait()


def ahead_kernel(pos, q_ref, k_ref, after, p_ref, low_ref):
    for i, h in enumerate(heads_of(k_ref.shape[-1])):
        shifted, factor = weights_of(q_ref[:, h], k_ref[:, h])
        attention = shifted * factor
        p_ref[i] = attention
        low_ref[i] = attention.astype(BF16)


def second_kernel(
    pos, q_ref, v_ref, came_ref, top_ref, dk_ref, dv_ref, p_ref, p_low_ref, *rest
):
    *waited, g_ref, ds_ref, low_ref = rest
    width = q_ref.shape[-1]
    g_ref[...] = jnp.where(pos[4] == 1, top_ref[...].astype(F32), came_ref[...].astype(F32)).astype(
        BF16
    )
    for i, h in enumerate(heads_of(width)):
        g = g_ref[:, h]
        attention_grad = dot(v_ref[:, h], g, NT)
        row_dot = jnp.sum(p_ref[i] * attention_grad, axis=0, keepdims=True)
        score_grad = (p_ref[i] * (attention_grad - row_dot)).astype(BF16)
        ds_ref[i] = score_grad
        dk = dk_ref[:, h] + dot(score_grad, q_ref[:, h], NN) * HEAD ** (-0.5)
        dv = dv_ref[:, h] + dot(p_low_ref[i], g, NN)
        low_ref[:, h] = dk.astype(BF16)
        low_ref[:, slice(width + h.start, width + h.stop)] = dv.astype(BF16)


def context_block(pos, step, half, low_ref, w_ref):
    width = w_ref.shape[-1] // 2
    count = low_ref.shape[0] // 2
    rows = slice(half * count, (half + 1) * count)
    return dot(rows_of(w_ref, (pos[0] + step) % NX, width), low_ref[rows, :], NT)


def context_kernel(half, steps, pos, low_ref, w_ref, *rest):
    out_ref = rest[-1]
    for i, step in enumerate(steps):
        out_ref[i] = context_block(pos, step, half, low_ref, w_ref).astype(BF16)


def across_kernel(pos, low_ref, w_ref, came_ref, after, top_ref, bottom_ref):
    total = context_block(pos, 2, 1, low_ref, w_ref) + came_ref[0].astype(F32)
    half = top_ref.shape[0]
    top_ref[...] = total[:half].astype(BF16)
    bottom_ref[...] = total[half:].astype(BF16)


def x_add_kernel(
    pos, keep_ref, came_ref, top_ref, bottom_ref, one_ref, after, late_one, next_ref, previous_ref
):
    late_one[...] = one_ref[...]
    half = top_ref.shape[0]
    next_ref[...] = (keep_ref[1].astype(F32) + came_ref[1].astype(F32)).astype(BF16)
    total = keep_ref[1, :half].astype(F32) + came_ref[1, :half].astype(F32)
    next_ref[:half] = (total + top_ref[...].astype(F32)).astype(BF16)
    previous_ref[...] = (keep_ref[2].astype(F32) + came_ref[2].astype(F32)).astype(BF16)
    total = keep_ref[2, half:].astype(F32) + came_ref[2, half:].astype(F32)
    previous_ref[half:] = (total + bottom_ref[...].astype(F32)).astype(BF16)


def z_add_kernel(pos, keep_ref, came_ref, b_ref, c_ref, text_a, text_b, two_ref, *outs):
    two_ref[0] = text_a[...]
    two_ref[1] = text_b[...]
    rows = outs[0].shape[0]
    width = outs[0].shape[1]
    for place in (slice(0, width // 2), slice(width // 2, width)):
        total = keep_ref[0, place, :].astype(F32) + came_ref[0, place, :].astype(F32)
        total = total + b_ref[place, :].astype(F32) + c_ref[place, :].astype(F32)
        total = total.T.astype(BF16)
        for j, out in enumerate(outs):
            out[:, place] = total[j * rows : (j + 1) * rows]


def third_kernel(pos, ds_ref, k_ref, w_ref, after, dq_ref, out_ref):
    for i, h in enumerate(heads_of(k_ref.shape[-1])):
        dq_ref[h, :] = (dot(k_ref[:, h], ds_ref[i], TN) * HEAD ** (-0.5)).astype(BF16)
    project_kernel(1, pos, dq_ref, w_ref, out_ref)


def z_sum_kernel(pos, a_ref, b_ref, c_ref, d_ref, keep_ref, send_ref):
    total = a_ref[...].astype(F32) + b_ref[...].astype(F32)
    total = total + c_ref[...].astype(F32) + d_ref[...].astype(F32)
    keep_ref[...] = total
    send_ref[...] = total.astype(BF16)


def core_sum_kernel(pos, keep_ref, came_ref, out_ref, send_ref):
    total = keep_ref[...] + came_ref[...].astype(F32)
    out_ref[...] = total
    send_ref[...] = total.astype(BF16)


def gather_kernel(pos, own, up, down, two, w_ref):
    rows = own.shape[1]
    places = (pos[1], pos[1] ^ 2, (pos[1] + 1) % NZ, (pos[1] + NZ - 1) % NZ)
    for ref, z in zip((own, two, up, down), places):
        for r in range(2):
            row = pl.multiple_of((z ^ (4 * r)) * rows, rows)
            w_ref[pl.ds(row, rows), :] = ref[r]


def text_kernel(pos, keep_ref, far_ref, w_ref, after, *rest):
    *outs, context_ref = rest
    context_ref[...] = (keep_ref[...] + far_ref[...].astype(F32)).astype(BF16)
    tokens = outs[0].shape[0]
    for i, out in enumerate(outs):
        row = pl.multiple_of((pos[0] + i) % NX * tokens, tokens)
        total = dot(context_ref[pl.ds(row, tokens), :], w_ref[...], NT)
        out[...] = total.astype(out.dtype)


def sent_kernel(pos, first_ref, g_ref, near_ref, far_ref, out_hbm, out_ref, sems):
    out_ref[0] = first_ref[...]
    total = (near_ref[...] + far_ref[...].astype(F32)).T
    out_ref[1] = (total + g_ref[...].astype(F32)).astype(BF16)
    copies([(out_ref, out_hbm)], sems)[0].wait()


def smooth_gate(inputs):
    return jax.nn.gelu(inputs, approximate=True)


def gelu_slope(inputs):
    unused_out, backward = jax.vjp(smooth_gate, inputs)
    return backward(jnp.ones_like(inputs))[0]


def shards(
    grad_in,
    grad_top,
    queries,
    keys,
    values,
    query_weight,
    key_weight,
    value_weight,
    text_weight,
    text_hidden,
):
    pos = positions()
    rows, width = grad_in.shape[1], grad_in.shape[2]
    text = keys.shape[1]
    heads = width // HEAD
    model = width * TENSOR
    where = (pos, pl.BlockSpec(memory_space=pltpu.SMEM))

    act = ((rows, width), BF16)
    turned = ((width, rows), BF16)
    pair = ((2, width, rows), BF16)
    square = ((text, width), F32)
    narrow = ((text, width), BF16)
    matrix = ((model, width), BF16)

    def vm(*shape_dtype):
        return pltpu.VMEM(*shape_dtype)

    def dma(count):
        return pltpu.SemaphoreType.DMA((count,))

    block = text_weight.shape

    dq0, wq, g_first = call(
        first_kernel,
        [where, (queries, HBM), (keys, HBM), (values, HBM), (grad_in, HBM), (query_weight, HBM)],
        [turned, matrix, act],
        [vm(*act), vm(*narrow), vm(*narrow), dma(9)],
    )
    def project(other, dq, *after):
        return call(
            functools.partial(project_kernel, other),
            [where, (dq, VMEM), (wq, VMEM)] + [(a, ANY) for a in after],
            [pair],
        )[0]

    send0 = project(1, dq0)
    came0 = swap_tensor(send0, 1)
    keep0 = project(0, dq0, send0)
    near0, far0 = call(
        meet_core_kernel,
        [where] + [(a, VMEM) for a in (keep0, came0)],
        [((width, rows), F32), turned],
    )
    far0_back = swap_tensor(far0, 2)

    dk0, dv0, q1, k, v, top, wkv = call(
        between_kernel,
        [
            where,
            (queries, HBM),
            (keys, HBM),
            (values, HBM),
            (grad_in, HBM),
            (grad_top, HBM),
            (key_weight, HBM),
            (value_weight, HBM),
            (far0, ANY),
        ],
        [square, square, act, narrow, narrow, act, ((model, 2 * width), BF16)],
        [vm(*act), vm(*act), dma(2 * SECTIONS + 6)],
    )

    sent0, text_one = call(
        meet_far_kernel,
        [where]
        + [(a, VMEM) for a in (g_first, near0, far0_back, turn(text_weight))]
        + [(dk0, ANY)],
        [act, (block, BF16)],
    )
    came_back = pass_back(sent0)
    p1, p1_low = call(
        ahead_kernel,
        [where, (q1, VMEM), (k, VMEM), (sent0, ANY)],
        [((heads, text, rows), F32), ((heads, text, rows), BF16)],
    )

    g1, ds1, low = call(
        second_kernel,
        [where] + [(a, VMEM) for a in (q1, v, came_back, top, dk0, dv0, p1, p1_low)],
        [act, ((heads, text, rows), BF16), ((text, 2 * width), BF16)],
    )

    def context_terms(half, steps, *after, flops=1):
        return call(
            functools.partial(context_kernel, half, steps),
            [where, (low, VMEM), (wkv, VMEM)] + [(a, ANY) for a in after],
            [((len(steps), width, text // 2), BF16)],
            flops=flops,
        )[0]

    near_steps = (0, 1, 3)
    send_across = context_terms(0, (2,))
    came_across = swap_tensor(send_across, 1)
    send = context_terms(0, near_steps, send_across)
    came = swap_tensor(send, 1)
    top, bottom = call(
        across_kernel,
        [where]
        + [(a, VMEM) for a in (low, wkv, came_across)]
        + [(send, ANY)],
        [((width // 2, text // 2), BF16)] * 2,
    )
    across = [send_x(top, 1), send_x(bottom, -1)]
    keep = context_terms(1, near_steps, top, flops=LONG)
    dq1, send1 = call(
        third_kernel,
        [where, (ds1, VMEM), (k, VMEM), (wq, VMEM), (keep, ANY)],
        [turned, pair],
    )
    came1 = swap_tensor(send1, 1)
    text_one, to_next, to_previous = call(
        x_add_kernel,
        [where] + [(a, VMEM) for a in (keep, came, *across, text_one)]
        + [(send1, ANY)],
        [(block, BF16)] + [((width, text // 2), BF16)] * 2,
        flops=LONG,
    )
    came_x = [send_x(to_next, 1), send_x(to_previous, -1)]
    text_across = swap_z(text_one, 4)

    keep1 = project(0, dq1, to_next)
    near1, far1 = call(
        meet_core_kernel,
        [where, (keep1, VMEM), (came1, VMEM)],
        [((width, rows), F32), turned],
    )
    others = (near1, swap_tensor(far1, 2))
    (sent,) = call(
        sent_kernel,
        [where, (sent0, VMEM), (g1, VMEM)] + [(a, VMEM) for a in others],
        [((2, rows, width), BF16)],
        [vm((2, rows, width), BF16), dma(1)],
        ANY,
    )

    few = text // NZ
    text_two, *by_z = call(
        z_add_kernel,
        [where] + [(a, VMEM) for a in (keep, came, *came_x, text_one, text_across)],
        [((2,) + block, BF16)] + [((few, width), BF16)] * (NZ // 2),
    )
    text_more = [from_z(text_two, 1), from_z(text_two, -1), swap_z(text_two, 2)]
    came_z = [send_z(by_z[i], i) for i in range(NZ // 2)]
    context, context_low = call(
        z_sum_kernel,
        [where] + [(a, VMEM) for a in came_z],
        [((few, width), F32), ((few, width), BF16)],
    )
    context, context_low = call(
        core_sum_kernel,
        [where, (context, VMEM), (swap_tensor(context_low, 1), VMEM)],
        [((few, width), F32), ((few, width), BF16)],
    )
    far_context = swap_tensor(context_low, 2)
    tokens = few // NX
    (gathered,) = call(
        gather_kernel,
        [where] + [(a, VMEM) for a in (text_two, *text_more)],
        [((width, width), BF16)],
    )
    hidden, *to_send = call(
        text_kernel,
        [where] + [(a, VMEM) for a in (context, far_context, gathered)] + [(sent, HBM)],
        [((tokens, width), F32)] + [((tokens, width), BF16)] * (NX - 1),
        [vm((few, width), BF16)],
    )
    for i, piece in enumerate(to_send):
        hidden = hidden + send_x(piece, i + 1).astype(F32)
    text_grad = hidden.T * gelu_slope(text_hidden.astype(F32))
    return (sent[None], text_grad)


def solution(mesh):
    placed = (
        P("section", "dp", "tensor"),
        P(None, "dp", "tensor"),
        P("section", None, "dp", "tensor"),
        P("section", "dp", "tensor"),
        P("section", "dp", "tensor"),
        P("section", None, "tensor"),
        P("section", None, "tensor"),
        P("section", None, "tensor"),
        P("section", "tensor"),
        P("tensor", ("dp", "section")),
    )
    return jax.shard_map(
        shards,
        mesh=mesh,
        in_specs=placed,
        out_specs=(P("section", None, "dp", "tensor"), P("tensor", ("dp", "section"))),
        check_vma=False,
    )
```

```python
import functools
import math

import jax
import jax.numpy as jnp
from jax import lax
from jax.experimental import pallas as pl
from jax.experimental.pallas import tpu as pltpu
from jax.sharding import PartitionSpec as P

HEAD = 128
NX, NZ = 4, 8
SECTIONS = NX * NZ
TENSOR = 4
LONG = 40_000_000_000
VMEM_LIMIT = 20 * 1024 * 1024
F32 = jnp.float32
BF16 = jnp.bfloat16
NT = (((1,), (1,)), ((), ()))
NN = (((1,), (0,)), ((), ()))
TN = (((0,), (0,)), ((), ()))


def dot(a, b, dims):
    return lax.dot_general(a, b, dims, preferred_element_type=F32)


def positions():
    section = lax.axis_index("section")
    tensor = lax.axis_index("tensor")
    return jnp.stack(
        [
            section // NZ,
            section % NZ,
            tensor // 2,
            tensor % 2,
            (section == SECTIONS - 1).astype(jnp.int32),
        ]
    ).astype(jnp.int32)


def block_for(pos, j, other):
    core = pos[3] ^ other
    return (pos[2] ^ (j % 2)) * 2 + (core ^ (j // 2))


def swap_tensor(value, bit):
    return lax.ppermute(value, "tensor", [(i, i ^ bit) for i in range(TENSOR)])


def send_x(value, step):
    pairs = [
        (x * NZ + z, ((x + step) % NX) * NZ + z) for x in range(NX) for z in range(NZ)
    ]
    return lax.ppermute(value, "section", pairs)


def send_z(value, step):
    pairs = []
    for x in range(NX):
        for z in range(NZ):
            for t in range(TENSOR):
                to = (z + step + 4 * (t % 2)) % NZ
                pairs.append(((x * NZ + z) * TENSOR + t, (x * NZ + to) * TENSOR + t))
    return lax.ppermute(value, ("section", "tensor"), pairs)


def turn(value):
    pairs = [
        ((x * NZ + z) * TENSOR + t, (t * NZ + z) * TENSOR + x)
        for x in range(NX)
        for z in range(NZ)
        for t in range(TENSOR)
    ]
    return lax.ppermute(value, ("section", "tensor"), pairs)


def swap_z(value, bits):
    pairs = [(s, s // NZ * NZ + ((s % NZ) ^ bits)) for s in range(SECTIONS)]
    return lax.ppermute(value, "section", pairs)


def from_z(value, step):
    pairs = [(s, s // NZ * NZ + (s - step) % NZ) for s in range(SECTIONS)]
    return lax.ppermute(value, "section", pairs)


def pass_back(value):
    return lax.ppermute(value, "section", [(s + 1, s) for s in range(SECTIONS - 1)])


def weights_of(q, k):
    factor = HEAD ** (-0.5) * math.log2(math.e)
    scores = dot(k, q, NT)
    peak = jnp.max(scores, axis=0, keepdims=True)
    shifted = jnp.exp2((scores - peak) * factor)
    return shifted, 1.0 / jnp.sum(shifted, axis=0, keepdims=True)


def score_gradient(shifted, factor, v, g):
    attention_grad = dot(v, g, NT)
    row_dot = jnp.sum(shifted * attention_grad, axis=0, keepdims=True) * factor
    return (shifted * (attention_grad * factor - row_dot * factor)).astype(BF16)


def heads_of(width):
    return [slice(i, i + HEAD) for i in range(0, width, HEAD)]

HBM = pl.BlockSpec(memory_space=pltpu.HBM)
VMEM = pl.BlockSpec(memory_space=pltpu.VMEM)
ANY = pl.BlockSpec(memory_space=pl.ANY)


def call(body, ins, outs, scratch=(), place=VMEM, flops=1):
    arrays = [
        pltpu.with_memory_space_constraint(array, pltpu.HBM) if spec is HBM else array
        for array, spec in ins
    ]
    shapes = [jax.ShapeDtypeStruct(*out) for out in outs]
    return pl.pallas_call(
        body,
        in_specs=[spec for array, spec in ins],
        out_specs=[place] * len(shapes),
        out_shape=shapes,
        scratch_shapes=list(scratch),
        compiler_params=pltpu.CompilerParams(vmem_limit_bytes=VMEM_LIMIT),
        cost_estimate=pl.CostEstimate(flops=flops, bytes_accessed=1, transcendentals=0),
    )(*arrays)


def copies(pairs, sems):
    started = []
    for i, (source, target) in enumerate(pairs):
        started.append(pltpu.make_async_copy(source, target, sems.at[i]))
        started[-1].start()
    return started


def rows_of(ref, block, count):
    return ref[pl.ds(pl.multiple_of(block * count, count), count), :]


def first_kernel(
    pos, q_hbm, k_hbm, v_hbm, g_hbm, w_hbm, dq_ref, w_ref, g_ref, q_ref, k_ref, v_ref, sems
):
    width = k_ref.shape[-1]
    heads = heads_of(width)
    refs = ((k_hbm.at[0], k_ref), (q_hbm.at[0, 0], q_ref), (v_hbm.at[0], v_ref), (g_hbm.at[0], g_ref))
    parts = (slice(0, HEAD), slice(HEAD, width))
    pairs = [(source.at[:, part], target.at[:, part]) for part in parts for source, target in refs]
    pairs.append((w_hbm.at[0], w_ref))
    started = copies(pairs, sems)
    for i, h in enumerate(heads):
        for copy in started[4 * i : 4 * i + 4] if i < 2 else ():
            copy.wait()
        k = k_ref[:, h]
        shifted, factor = weights_of(q_ref[:, h], k)
        score_grad = score_gradient(shifted, factor, v_ref[:, h], g_ref[:, h])
        dq_ref[h, :] = (dot(k, score_grad, TN) * HEAD ** (-0.5)).astype(BF16)
    started[-1].wait()


def project_kernel(other, pos, dq_ref, w_ref, *rest):
    out_ref = rest[-1]
    width = w_ref.shape[-1]
    for j in range(2):
        weight = rows_of(w_ref, block_for(pos, j, other), width)
        out_ref[j] = dot(weight, dq_ref[...], NN).astype(BF16)


def meet_core_kernel(pos, keep_ref, came_ref, near_ref, far_ref):
    near_ref[...] = keep_ref[0].astype(F32) + came_ref[0].astype(F32)
    far_ref[...] = (keep_ref[1].astype(F32) + came_ref[1].astype(F32)).astype(BF16)


def meet_far_kernel(pos, g_ref, near_ref, far_ref, text, after, out_ref, text_ref):
    text_ref[...] = text[...]
    total = (near_ref[...] + far_ref[...].astype(F32)).T
    out_ref[...] = (total + g_ref[...].astype(F32)).astype(BF16)


def between_kernel(
    pos,
    q_hbm,
    k_hbm,
    v_hbm,
    g_hbm,
    top_hbm,
    wk_hbm,
    wv_hbm,
    after,
    dk_ref,
    dv_ref,
    q_ref,
    k_ref,
    v_ref,
    top_ref,
    wkv_ref,
    q0_ref,
    g_ref,
    sems,
):
    pairs = [(q_hbm.at[0, 0], q0_ref), (g_hbm.at[0], g_ref)]
    rows = k_ref.shape[0] // SECTIONS
    for other in range(2):
        core = pos[3] ^ (1 - other)
        for kz in range(NZ // 2):
            to_z = (pos[1] + kz + 4 * core) % NZ
            for to_x in range(NX):
                source = pl.ds(pl.multiple_of((to_x * NZ + to_z) * rows, rows), rows)
                place = pl.ds(((other * (NZ // 2) + kz) * NX + to_x) * rows, rows)
                pairs.append((k_hbm.at[0, source], k_ref.at[place]))
                pairs.append((v_hbm.at[0, source], v_ref.at[place]))
    first = len(pairs)
    pairs.append((q_hbm.at[0, 1], q_ref))
    pairs.append((top_hbm.at[0], top_ref))
    width = k_ref.shape[-1]
    pairs.append((wk_hbm.at[0], wkv_ref.at[:, :width]))
    pairs.append((wv_hbm.at[0], wkv_ref.at[:, width:]))
    started = copies(pairs, sems)
    for copy in started[:first]:
        copy.wait()
    for h in heads_of(k_ref.shape[-1]):
        q = q0_ref[:, h]
        g = g_ref[:, h]
        shifted, factor = weights_of(q, k_ref[:, h])
        score_grad = score_gradient(shifted, factor, v_ref[:, h], g)
        dk_ref[:, h] = dot(score_grad, q, NN) * HEAD ** (-0.5)
        dv_ref[:, h] = dot((shifted * factor).astype(BF16), g, NN)
    for copy in started[first:]:
        copy.wait()


def ahead_kernel(pos, q_ref, k_ref, one_ref, after, p_ref, low_ref, late_one):
    late_one[...] = one_ref[...]
    for i, h in enumerate(heads_of(k_ref.shape[-1])):
        shifted, factor = weights_of(q_ref[:, h], k_ref[:, h])
        attention = shifted * factor
        p_ref[i] = attention
        low_ref[i] = attention.astype(BF16)


def second_kernel(
    pos, q_ref, v_ref, came_ref, top_ref, dk_ref, dv_ref, p_ref, p_low_ref, *rest
):
    *waited, g_ref, ds_ref, low_ref = rest
    width = q_ref.shape[-1]
    g_ref[...] = jnp.where(pos[4] == 1, top_ref[...].astype(F32), came_ref[...].astype(F32)).astype(
        BF16
    )
    for i, h in enumerate(heads_of(width)):
        g = g_ref[:, h]
        attention_grad = dot(v_ref[:, h], g, NT)
        row_dot = jnp.sum(p_ref[i] * attention_grad, axis=0, keepdims=True)
        score_grad = (p_ref[i] * (attention_grad - row_dot)).astype(BF16)
        ds_ref[i] = score_grad
        dk = dk_ref[:, h] + dot(score_grad, q_ref[:, h], NN) * HEAD ** (-0.5)
        dv = dv_ref[:, h] + dot(p_low_ref[i], g, NN)
        low_ref[:, h] = dk.astype(BF16)
        low_ref[:, slice(width + h.start, width + h.stop)] = dv.astype(BF16)


def context_block(pos, step, half, low_ref, w_ref):
    width = w_ref.shape[-1] // 2
    count = low_ref.shape[0] // 2
    rows = slice(half * count, (half + 1) * count)
    return dot(rows_of(w_ref, (pos[0] + step) % NX, width), low_ref[rows, :], NT)


def context_kernel(half, steps, pos, low_ref, w_ref, *rest):
    out_ref = rest[-1]
    for i, step in enumerate(steps):
        out_ref[i] = context_block(pos, step, half, low_ref, w_ref).astype(BF16)


def across_kernel(pos, low_ref, w_ref, came_ref, after, top_ref, bottom_ref):
    total = context_block(pos, 2, 1, low_ref, w_ref) + came_ref[0].astype(F32)
    half = top_ref.shape[0]
    top_ref[...] = total[:half].astype(BF16)
    bottom_ref[...] = total[half:].astype(BF16)


def x_add_kernel(
    pos, keep_ref, came_ref, top_ref, bottom_ref, text_a, text_b, after, two_ref, next_ref, previous_ref
):
    two_ref[0] = text_a[...]
    two_ref[1] = text_b[...]
    half = top_ref.shape[0]
    next_ref[...] = (keep_ref[1].astype(F32) + came_ref[1].astype(F32)).astype(BF16)
    total = keep_ref[1, :half].astype(F32) + came_ref[1, :half].astype(F32)
    next_ref[:half] = (total + top_ref[...].astype(F32)).astype(BF16)
    previous_ref[...] = (keep_ref[2].astype(F32) + came_ref[2].astype(F32)).astype(BF16)
    total = keep_ref[2, half:].astype(F32) + came_ref[2, half:].astype(F32)
    previous_ref[half:] = (total + bottom_ref[...].astype(F32)).astype(BF16)


def z_add_kernel(pos, keep_ref, came_ref, b_ref, c_ref, text, two_ref, *outs):
    two_ref[...] = text[...]
    rows = outs[0].shape[0]
    width = outs[0].shape[1]
    for place in (slice(0, width // 2), slice(width // 2, width)):
        total = keep_ref[0, place, :].astype(F32) + came_ref[0, place, :].astype(F32)
        total = total + b_ref[place, :].astype(F32) + c_ref[place, :].astype(F32)
        total = total.T.astype(BF16)
        for j, out in enumerate(outs):
            out[:, place] = total[j * rows : (j + 1) * rows]


def third_kernel(pos, ds_ref, k_ref, w_ref, after, dq_ref, out_ref):
    for i, h in enumerate(heads_of(k_ref.shape[-1])):
        dq_ref[h, :] = (dot(k_ref[:, h], ds_ref[i], TN) * HEAD ** (-0.5)).astype(BF16)
    project_kernel(1, pos, dq_ref, w_ref, out_ref)


def z_sum_kernel(pos, a_ref, b_ref, c_ref, d_ref, after, keep_ref, send_ref):
    total = a_ref[...].astype(F32) + b_ref[...].astype(F32)
    total = total + c_ref[...].astype(F32) + d_ref[...].astype(F32)
    keep_ref[...] = total
    send_ref[...] = total.astype(BF16)


def core_sum_kernel(pos, keep_ref, came_ref, out_ref, send_ref):
    total = keep_ref[...] + came_ref[...].astype(F32)
    out_ref[...] = total
    send_ref[...] = total.astype(BF16)


def gather_kernel(pos, own, up, down, two, w_ref):
    rows = own.shape[1]
    places = (pos[1], pos[1] ^ 2, (pos[1] + 1) % NZ, (pos[1] + NZ - 1) % NZ)
    for ref, z in zip((own, two, up, down), places):
        for r in range(2):
            row = pl.multiple_of((z ^ (4 * r)) * rows, rows)
            w_ref[pl.ds(row, rows), :] = ref[r]


def text_kernel(pos, keep_ref, far_ref, w_ref, after, *rest):
    *outs, total_ref = rest
    context = (keep_ref[...] + far_ref[...].astype(F32)).astype(BF16)
    total_ref[...] = dot(context, w_ref[...], NT)
    tokens = outs[0].shape[0]
    for i, out in enumerate(outs):
        row = pl.multiple_of((pos[0] + i) % NX * tokens, tokens)
        out[...] = total_ref[pl.ds(row, tokens), :].astype(out.dtype)


def sent_kernel(pos, first_ref, g_ref, near_ref, far_ref, out_hbm, out_ref, sems):
    out_ref[0] = first_ref[...]
    total = (near_ref[...] + far_ref[...].astype(F32)).T
    out_ref[1] = (total + g_ref[...].astype(F32)).astype(BF16)
    copies([(out_ref, out_hbm)], sems)[0].wait()


def smooth_gate(inputs):
    return jax.nn.gelu(inputs, approximate=True)


def gelu_slope(inputs):
    unused_out, backward = jax.vjp(smooth_gate, inputs)
    return backward(jnp.ones_like(inputs))[0]


def shards(
    grad_in,
    grad_top,
    queries,
    keys,
    values,
    query_weight,
    key_weight,
    value_weight,
    text_weight,
    text_hidden,
):
    pos = positions()
    rows, width = grad_in.shape[1], grad_in.shape[2]
    text = keys.shape[1]
    heads = width // HEAD
    model = width * TENSOR
    where = (pos, pl.BlockSpec(memory_space=pltpu.SMEM))

    act = ((rows, width), BF16)
    turned = ((width, rows), BF16)
    pair = ((2, width, rows), BF16)
    square = ((text, width), F32)
    narrow = ((text, width), BF16)
    matrix = ((model, width), BF16)

    def vm(*shape_dtype):
        return pltpu.VMEM(*shape_dtype)

    def dma(count):
        return pltpu.SemaphoreType.DMA((count,))

    block = text_weight.shape

    dq0, wq, g_first = call(
        first_kernel,
        [where, (queries, HBM), (keys, HBM), (values, HBM), (grad_in, HBM), (query_weight, HBM)],
        [turned, matrix, act],
        [vm(*act), vm(*narrow), vm(*narrow), dma(9)],
    )
    def project(other, dq, *after):
        return call(
            functools.partial(project_kernel, other),
            [where, (dq, VMEM), (wq, VMEM)] + [(a, ANY) for a in after],
            [pair],
        )[0]

    send0 = project(1, dq0)
    came0 = swap_tensor(send0, 1)
    keep0 = project(0, dq0, send0)
    near0, far0 = call(
        meet_core_kernel,
        [where] + [(a, VMEM) for a in (keep0, came0)],
        [((width, rows), F32), turned],
    )
    far0_back = swap_tensor(far0, 2)

    dk0, dv0, q1, k, v, top, wkv = call(
        between_kernel,
        [
            where,
            (queries, HBM),
            (keys, HBM),
            (values, HBM),
            (grad_in, HBM),
            (grad_top, HBM),
            (key_weight, HBM),
            (value_weight, HBM),
            (far0, ANY),
        ],
        [square, square, act, narrow, narrow, act, ((model, 2 * width), BF16)],
        [vm(*act), vm(*act), dma(2 * SECTIONS + 6)],
    )

    sent0, text_one = call(
        meet_far_kernel,
        [where]
        + [(a, VMEM) for a in (g_first, near0, far0_back, turn(text_weight))]
        + [(dk0, ANY)],
        [act, (block, BF16)],
    )
    came_back = pass_back(sent0)
    p1, p1_low, text_one = call(
        ahead_kernel,
        [where, (q1, VMEM), (k, VMEM), (text_one, VMEM), (sent0, ANY)],
        [((heads, text, rows), F32), ((heads, text, rows), BF16), (block, BF16)],
    )
    text_across = swap_z(text_one, 4)

    g1, ds1, low = call(
        second_kernel,
        [where] + [(a, VMEM) for a in (q1, v, came_back, top, dk0, dv0, p1, p1_low)],
        [act, ((heads, text, rows), BF16), ((text, 2 * width), BF16)],
    )

    def context_terms(half, steps, *after, flops=1):
        return call(
            functools.partial(context_kernel, half, steps),
            [where, (low, VMEM), (wkv, VMEM)] + [(a, ANY) for a in after],
            [((len(steps), width, text // 2), BF16)],
            flops=flops,
        )[0]

    near_steps = (0, 1, 3)
    send_across = context_terms(0, (2,), text_across)
    came_across = swap_tensor(send_across, 1)
    send = context_terms(0, near_steps, send_across)
    came = swap_tensor(send, 1)
    top, bottom = call(
        across_kernel,
        [where]
        + [(a, VMEM) for a in (low, wkv, came_across)]
        + [(send, ANY)],
        [((width // 2, text // 2), BF16)] * 2,
    )
    across = [send_x(top, 1), send_x(bottom, -1)]
    keep = context_terms(1, near_steps, top, flops=LONG)
    dq1, send1 = call(
        third_kernel,
        [where, (ds1, VMEM), (k, VMEM), (wq, VMEM), (keep, ANY)],
        [turned, pair],
    )
    came1 = swap_tensor(send1, 1)
    text_two, to_next, to_previous = call(
        x_add_kernel,
        [where] + [(a, VMEM) for a in (keep, came, *across, text_one, text_across)]
        + [(send1, ANY)],
        [((2,) + block, BF16)] + [((width, text // 2), BF16)] * 2,
        flops=LONG,
    )
    text_second = swap_z(text_two, 2)
    came_x = [send_x(to_next, 1), send_x(to_previous, -1)]

    keep1 = project(0, dq1, to_next)
    near1, far1 = call(
        meet_core_kernel,
        [where, (keep1, VMEM), (came1, VMEM)],
        [((width, rows), F32), turned],
    )
    others = (near1, swap_tensor(far1, 2))
    (sent,) = call(
        sent_kernel,
        [where, (sent0, VMEM), (g1, VMEM)] + [(a, VMEM) for a in others],
        [((2, rows, width), BF16)],
        [vm((2, rows, width), BF16), dma(1)],
        ANY,
    )

    few = text // NZ
    text_two, *by_z = call(
        z_add_kernel,
        [where] + [(a, VMEM) for a in (keep, came, *came_x, text_two)],
        [((2,) + block, BF16)] + [((few, width), BF16)] * (NZ // 2),
    )
    text_more = [from_z(text_two, 1), from_z(text_two, -1), text_second]
    came_z = [send_z(by_z[i], i) for i in range(NZ // 2)]
    context, context_low = call(
        z_sum_kernel,
        [where] + [(a, VMEM) for a in came_z] + [(text_second, ANY)],
        [((few, width), F32), ((few, width), BF16)],
    )
    context, context_low = call(
        core_sum_kernel,
        [where, (context, VMEM), (swap_tensor(context_low, 1), VMEM)],
        [((few, width), F32), ((few, width), BF16)],
    )
    far_context = swap_tensor(context_low, 2)
    tokens = few // NX
    (gathered,) = call(
        gather_kernel,
        [where] + [(a, VMEM) for a in (text_two, *text_more)],
        [((width, width), BF16)],
    )
    hidden, *to_send = call(
        text_kernel,
        [where] + [(a, VMEM) for a in (context, far_context, gathered)] + [(sent, HBM)],
        [((tokens, width), F32)] + [((tokens, width), BF16)] * (NX - 1),
        [vm((few, width), F32)],
    )
    for i, piece in enumerate(to_send):
        hidden = hidden + send_x(piece, i + 1).astype(F32)
    text_grad = hidden.T * gelu_slope(text_hidden.astype(F32))
    return (sent[None], text_grad)


def solution(mesh):
    placed = (
        P("section", "dp", "tensor"),
        P(None, "dp", "tensor"),
        P("section", None, "dp", "tensor"),
        P("section", "dp", "tensor"),
        P("section", "dp", "tensor"),
        P("section", None, "tensor"),
        P("section", None, "tensor"),
        P("section", None, "tensor"),
        P("section", "tensor"),
        P("tensor", ("dp", "section")),
    )
    return jax.shard_map(
        shards,
        mesh=mesh,
        in_specs=placed,
        out_specs=(P("section", None, "dp", "tensor"), P("tensor", ("dp", "section"))),
        check_vma=False,
    )
```

```python
import functools
import math

import jax
import jax.numpy as jnp
from jax import lax
from jax.experimental import pallas as pl
from jax.experimental.pallas import tpu as pltpu
from jax.sharding import PartitionSpec as P

HEAD = 128
NX, NZ = 4, 8
SECTIONS = NX * NZ
TENSOR = 4
LONG = 40_000_000_000
VMEM_LIMIT = 20 * 1024 * 1024
F32 = jnp.float32
BF16 = jnp.bfloat16
NT = (((1,), (1,)), ((), ()))
NN = (((1,), (0,)), ((), ()))
TN = (((0,), (0,)), ((), ()))


def dot(a, b, dims):
    return lax.dot_general(a, b, dims, preferred_element_type=F32)


def positions():
    section = lax.axis_index("section")
    tensor = lax.axis_index("tensor")
    return jnp.stack(
        [
            section // NZ,
            section % NZ,
            tensor // 2,
            tensor % 2,
            (section == SECTIONS - 1).astype(jnp.int32),
        ]
    ).astype(jnp.int32)


def block_for(pos, j, other):
    core = pos[3] ^ other
    return (pos[2] ^ (j % 2)) * 2 + (core ^ (j // 2))


def swap_tensor(value, bit):
    return lax.ppermute(value, "tensor", [(i, i ^ bit) for i in range(TENSOR)])


def send_x(value, step):
    pairs = [
        (x * NZ + z, ((x + step) % NX) * NZ + z) for x in range(NX) for z in range(NZ)
    ]
    return lax.ppermute(value, "section", pairs)


def send_z(value, step):
    pairs = []
    for x in range(NX):
        for z in range(NZ):
            for t in range(TENSOR):
                to = (z + step + 4 * (t % 2)) % NZ
                pairs.append(((x * NZ + z) * TENSOR + t, (x * NZ + to) * TENSOR + t))
    return lax.ppermute(value, ("section", "tensor"), pairs)


def turn(value):
    pairs = [
        ((x * NZ + z) * TENSOR + t, (t * NZ + z) * TENSOR + x)
        for x in range(NX)
        for z in range(NZ)
        for t in range(TENSOR)
    ]
    return lax.ppermute(value, ("section", "tensor"), pairs)


def swap_z(value, bits):
    pairs = [(s, s // NZ * NZ + ((s % NZ) ^ bits)) for s in range(SECTIONS)]
    return lax.ppermute(value, "section", pairs)


def from_z(value, step):
    pairs = [(s, s // NZ * NZ + (s - step) % NZ) for s in range(SECTIONS)]
    return lax.ppermute(value, "section", pairs)


def pass_back(value):
    return lax.ppermute(value, "section", [(s + 1, s) for s in range(SECTIONS - 1)])


def weights_of(q, k):
    factor = HEAD ** (-0.5) * math.log2(math.e)
    scores = dot(k, q, NT)
    peak = jnp.max(scores, axis=0, keepdims=True)
    shifted = jnp.exp2((scores - peak) * factor)
    return shifted, 1.0 / jnp.sum(shifted, axis=0, keepdims=True)


def score_gradient(shifted, factor, v, g):
    attention_grad = dot(v, g, NT)
    row_dot = jnp.sum(shifted * attention_grad, axis=0, keepdims=True) * factor
    return (shifted * (attention_grad * factor - row_dot * factor)).astype(BF16)


def heads_of(width):
    return [slice(i, i + HEAD) for i in range(0, width, HEAD)]

HBM = pl.BlockSpec(memory_space=pltpu.HBM)
VMEM = pl.BlockSpec(memory_space=pltpu.VMEM)
ANY = pl.BlockSpec(memory_space=pl.ANY)


def call(body, ins, outs, scratch=(), place=VMEM, flops=1):
    arrays = [
        pltpu.with_memory_space_constraint(array, pltpu.HBM) if spec is HBM else array
        for array, spec in ins
    ]
    shapes = [jax.ShapeDtypeStruct(*out) for out in outs]
    return pl.pallas_call(
        body,
        in_specs=[spec for array, spec in ins],
        out_specs=[place] * len(shapes),
        out_shape=shapes,
        scratch_shapes=list(scratch),
        compiler_params=pltpu.CompilerParams(vmem_limit_bytes=VMEM_LIMIT),
        cost_estimate=pl.CostEstimate(flops=flops, bytes_accessed=1, transcendentals=0),
    )(*arrays)


def copies(pairs, sems):
    started = []
    for i, (source, target) in enumerate(pairs):
        started.append(pltpu.make_async_copy(source, target, sems.at[i]))
        started[-1].start()
    return started


def rows_of(ref, block, count):
    return ref[pl.ds(pl.multiple_of(block * count, count), count), :]


def first_kernel(
    pos, q_hbm, k_hbm, v_hbm, g_hbm, w_hbm, dq_ref, w_ref, g_ref, q_ref, k_ref, v_ref, sems
):
    width = k_ref.shape[-1]
    heads = heads_of(width)
    refs = ((k_hbm.at[0], k_ref), (q_hbm.at[0, 0], q_ref), (v_hbm.at[0], v_ref), (g_hbm.at[0], g_ref))
    parts = (slice(0, HEAD), slice(HEAD, width))
    pairs = [(source.at[:, part], target.at[:, part]) for part in parts for source, target in refs]
    pairs.append((w_hbm.at[0], w_ref))
    started = copies(pairs, sems)
    for i, h in enumerate(heads):
        for copy in started[4 * i : 4 * i + 4] if i < 2 else ():
            copy.wait()
        k = k_ref[:, h]
        shifted, factor = weights_of(q_ref[:, h], k)
        score_grad = score_gradient(shifted, factor, v_ref[:, h], g_ref[:, h])
        dq_ref[h, :] = (dot(k, score_grad, TN) * HEAD ** (-0.5)).astype(BF16)
    started[-1].wait()


def project_kernel(other, pos, dq_ref, w_ref, *rest):
    out_ref = rest[-1]
    width = w_ref.shape[-1]
    for j in range(2):
        weight = rows_of(w_ref, block_for(pos, j, other), width)
        out_ref[j] = dot(weight, dq_ref[...], NN).astype(BF16)


def meet_core_kernel(pos, keep_ref, came_ref, near_ref, far_ref):
    near_ref[...] = keep_ref[0].astype(F32) + came_ref[0].astype(F32)
    far_ref[...] = (keep_ref[1].astype(F32) + came_ref[1].astype(F32)).astype(BF16)


def meet_far_kernel(pos, g_ref, near_ref, far_ref, text, after, out_ref, text_ref):
    text_ref[...] = text[...]
    total = (near_ref[...] + far_ref[...].astype(F32)).T
    out_ref[...] = (total + g_ref[...].astype(F32)).astype(BF16)


def between_kernel(
    pos,
    q_hbm,
    k_hbm,
    v_hbm,
    g_hbm,
    top_hbm,
    wk_hbm,
    wv_hbm,
    after,
    dk_ref,
    dv_ref,
    q_ref,
    k_ref,
    v_ref,
    top_ref,
    wkv_ref,
    q0_ref,
    g_ref,
    sems,
):
    pairs = [(q_hbm.at[0, 0], q0_ref), (g_hbm.at[0], g_ref)]
    rows = k_ref.shape[0] // SECTIONS
    for other in range(2):
        core = pos[3] ^ (1 - other)
        for kz in range(NZ // 2):
            to_z = (pos[1] + kz + 4 * core) % NZ
            for to_x in range(NX):
                source = pl.ds(pl.multiple_of((to_x * NZ + to_z) * rows, rows), rows)
                place = pl.ds(((other * (NZ // 2) + kz) * NX + to_x) * rows, rows)
                pairs.append((k_hbm.at[0, source], k_ref.at[place]))
                pairs.append((v_hbm.at[0, source], v_ref.at[place]))
    first = len(pairs)
    pairs.append((q_hbm.at[0, 1], q_ref))
    pairs.append((top_hbm.at[0], top_ref))
    width = k_ref.shape[-1]
    pairs.append((wk_hbm.at[0], wkv_ref.at[:, :width]))
    pairs.append((wv_hbm.at[0], wkv_ref.at[:, width:]))
    started = copies(pairs, sems)
    for copy in started[:first]:
        copy.wait()
    for h in heads_of(k_ref.shape[-1]):
        q = q0_ref[:, h]
        g = g_ref[:, h]
        shifted, factor = weights_of(q, k_ref[:, h])
        score_grad = score_gradient(shifted, factor, v_ref[:, h], g)
        dk_ref[:, h] = dot(score_grad, q, NN) * HEAD ** (-0.5)
        dv_ref[:, h] = dot((shifted * factor).astype(BF16), g, NN)
    for copy in started[first:]:
        copy.wait()


def ahead_kernel(pos, q_ref, k_ref, one_ref, after, p_ref, low_ref, late_one):
    late_one[...] = one_ref[...]
    for i, h in enumerate(heads_of(k_ref.shape[-1])):
        shifted, factor = weights_of(q_ref[:, h], k_ref[:, h])
        attention = shifted * factor
        p_ref[i] = attention
        low_ref[i] = attention.astype(BF16)


def mix_kernel(pos, p_low_ref, v_ref, mixed_ref):
    for i, h in enumerate(heads_of(v_ref.shape[-1])):
        mixed_ref[h, :] = dot(v_ref[:, h], p_low_ref[i], TN)


def second_kernel(
    pos, q_ref, v_ref, came_ref, top_ref, dk_ref, dv_ref, p_ref, p_low_ref, mixed_ref, *rest
):
    *waited, g_ref, ds_ref, low_ref = rest
    width = q_ref.shape[-1]
    g_ref[...] = jnp.where(pos[4] == 1, top_ref[...].astype(F32), came_ref[...].astype(F32)).astype(
        BF16
    )
    for i, h in enumerate(heads_of(width)):
        g = g_ref[:, h]
        attention_grad = dot(v_ref[:, h], g, NT)
        row_dot = jnp.sum(mixed_ref[h, :] * g.astype(F32).T, axis=0, keepdims=True)
        score_grad = (p_ref[i] * (attention_grad - row_dot)).astype(BF16)
        ds_ref[i] = score_grad
        dk = dk_ref[:, h] + dot(score_grad, q_ref[:, h], NN) * HEAD ** (-0.5)
        dv = dv_ref[:, h] + dot(p_low_ref[i], g, NN)
        low_ref[:, h] = dk.astype(BF16)
        low_ref[:, slice(width + h.start, width + h.stop)] = dv.astype(BF16)


def context_block(pos, step, half, low_ref, w_ref):
    width = w_ref.shape[-1] // 2
    count = low_ref.shape[0] // 2
    rows = slice(half * count, (half + 1) * count)
    return dot(rows_of(w_ref, (pos[0] + step) % NX, width), low_ref[rows, :], NT)


def context_kernel(half, steps, pos, low_ref, w_ref, *rest):
    out_ref = rest[-1]
    for i, step in enumerate(steps):
        out_ref[i] = context_block(pos, step, half, low_ref, w_ref).astype(BF16)


def across_kernel(pos, low_ref, w_ref, came_ref, after, top_ref, bottom_ref):
    total = context_block(pos, 2, 1, low_ref, w_ref) + came_ref[0].astype(F32)
    half = top_ref.shape[0]
    top_ref[...] = total[:half].astype(BF16)
    bottom_ref[...] = total[half:].astype(BF16)


def x_add_kernel(
    pos, keep_ref, came_ref, top_ref, bottom_ref, text_a, text_b, after, two_ref, next_ref, previous_ref
):
    two_ref[0] = text_a[...]
    two_ref[1] = text_b[...]
    half = top_ref.shape[0]
    next_ref[...] = (keep_ref[1].astype(F32) + came_ref[1].astype(F32)).astype(BF16)
    total = keep_ref[1, :half].astype(F32) + came_ref[1, :half].astype(F32)
    next_ref[:half] = (total + top_ref[...].astype(F32)).astype(BF16)
    previous_ref[...] = (keep_ref[2].astype(F32) + came_ref[2].astype(F32)).astype(BF16)
    total = keep_ref[2, half:].astype(F32) + came_ref[2, half:].astype(F32)
    previous_ref[half:] = (total + bottom_ref[...].astype(F32)).astype(BF16)


def z_add_kernel(pos, keep_ref, came_ref, b_ref, c_ref, text, two_ref, *outs):
    two_ref[...] = text[...]
    rows = outs[0].shape[0]
    width = outs[0].shape[1]
    for place in (slice(0, width // 2), slice(width // 2, width)):
        total = keep_ref[0, place, :].astype(F32) + came_ref[0, place, :].astype(F32)
        total = total + b_ref[place, :].astype(F32) + c_ref[place, :].astype(F32)
        total = total.T.astype(BF16)
        for j, out in enumerate(outs):
            out[:, place] = total[j * rows : (j + 1) * rows]


def third_kernel(pos, ds_ref, k_ref, w_ref, after, dq_ref, out_ref):
    for i, h in enumerate(heads_of(k_ref.shape[-1])):
        dq_ref[h, :] = (dot(k_ref[:, h], ds_ref[i], TN) * HEAD ** (-0.5)).astype(BF16)
    project_kernel(1, pos, dq_ref, w_ref, out_ref)


def z_sum_kernel(pos, a_ref, b_ref, c_ref, d_ref, after, keep_ref, send_ref):
    total = a_ref[...].astype(F32) + b_ref[...].astype(F32)
    total = total + c_ref[...].astype(F32) + d_ref[...].astype(F32)
    keep_ref[...] = total
    send_ref[...] = total.astype(BF16)


def core_sum_kernel(pos, keep_ref, came_ref, out_ref, send_ref):
    total = keep_ref[...] + came_ref[...].astype(F32)
    out_ref[...] = total
    send_ref[...] = total.astype(BF16)


def gather_kernel(pos, own, up, down, two, w_ref):
    rows = own.shape[1]
    places = (pos[1], pos[1] ^ 2, (pos[1] + 1) % NZ, (pos[1] + NZ - 1) % NZ)
    for ref, z in zip((own, two, up, down), places):
        for r in range(2):
            row = pl.multiple_of((z ^ (4 * r)) * rows, rows)
            w_ref[pl.ds(row, rows), :] = ref[r]


def text_kernel(pos, keep_ref, far_ref, w_ref, after, *rest):
    *outs, total_ref = rest
    context = (keep_ref[...] + far_ref[...].astype(F32)).astype(BF16)
    total_ref[...] = dot(context, w_ref[...], NT)
    tokens = outs[0].shape[0]
    for i, out in enumerate(outs):
        row = pl.multiple_of((pos[0] + i) % NX * tokens, tokens)
        out[...] = total_ref[pl.ds(row, tokens), :].astype(out.dtype)


def sent_kernel(pos, first_ref, g_ref, near_ref, far_ref, out_hbm, out_ref, sems):
    out_ref[0] = first_ref[...]
    total = (near_ref[...] + far_ref[...].astype(F32)).T
    out_ref[1] = (total + g_ref[...].astype(F32)).astype(BF16)
    copies([(out_ref, out_hbm)], sems)[0].wait()


def smooth_gate(inputs):
    return jax.nn.gelu(inputs, approximate=True)


def gelu_slope(inputs):
    unused_out, backward = jax.vjp(smooth_gate, inputs)
    return backward(jnp.ones_like(inputs))[0]


def shards(
    grad_in,
    grad_top,
    queries,
    keys,
    values,
    query_weight,
    key_weight,
    value_weight,
    text_weight,
    text_hidden,
):
    pos = positions()
    rows, width = grad_in.shape[1], grad_in.shape[2]
    text = keys.shape[1]
    heads = width // HEAD
    model = width * TENSOR
    where = (pos, pl.BlockSpec(memory_space=pltpu.SMEM))

    act = ((rows, width), BF16)
    turned = ((width, rows), BF16)
    pair = ((2, width, rows), BF16)
    square = ((text, width), F32)
    narrow = ((text, width), BF16)
    matrix = ((model, width), BF16)

    def vm(*shape_dtype):
        return pltpu.VMEM(*shape_dtype)

    def dma(count):
        return pltpu.SemaphoreType.DMA((count,))

    block = text_weight.shape

    dq0, wq, g_first = call(
        first_kernel,
        [where, (queries, HBM), (keys, HBM), (values, HBM), (grad_in, HBM), (query_weight, HBM)],
        [turned, matrix, act],
        [vm(*act), vm(*narrow), vm(*narrow), dma(9)],
    )
    def project(other, dq, *after):
        return call(
            functools.partial(project_kernel, other),
            [where, (dq, VMEM), (wq, VMEM)] + [(a, ANY) for a in after],
            [pair],
        )[0]

    send0 = project(1, dq0)
    came0 = swap_tensor(send0, 1)
    keep0 = project(0, dq0, send0)
    near0, far0 = call(
        meet_core_kernel,
        [where] + [(a, VMEM) for a in (keep0, came0)],
        [((width, rows), F32), turned],
    )
    far0_back = swap_tensor(far0, 2)

    dk0, dv0, q1, k, v, top, wkv = call(
        between_kernel,
        [
            where,
            (queries, HBM),
            (keys, HBM),
            (values, HBM),
            (grad_in, HBM),
            (grad_top, HBM),
            (key_weight, HBM),
            (value_weight, HBM),
            (far0, ANY),
        ],
        [square, square, act, narrow, narrow, act, ((model, 2 * width), BF16)],
        [vm(*act), vm(*act), dma(2 * SECTIONS + 6)],
    )

    sent0, text_one = call(
        meet_far_kernel,
        [where]
        + [(a, VMEM) for a in (g_first, near0, far0_back, turn(text_weight))]
        + [(dk0, ANY)],
        [act, (block, BF16)],
    )
    came_back = pass_back(sent0)
    p1, p1_low, text_one = call(
        ahead_kernel,
        [where] + [(a, VMEM) for a in (q1, k, text_one)] + [(sent0, ANY)],
        [((heads, text, rows), F32), ((heads, text, rows), BF16), (block, BF16)],
    )
    text_across = swap_z(text_one, 4)
    (mixed,) = call(mix_kernel, [where, (p1_low, VMEM), (v, VMEM)], [((width, rows), F32)])

    g1, ds1, low = call(
        second_kernel,
        [where] + [(a, VMEM) for a in (q1, v, came_back, top, dk0, dv0, p1, p1_low, mixed)],
        [act, ((heads, text, rows), BF16), ((text, 2 * width), BF16)],
    )

    def context_terms(half, steps, *after, flops=1):
        return call(
            functools.partial(context_kernel, half, steps),
            [where, (low, VMEM), (wkv, VMEM)] + [(a, ANY) for a in after],
            [((len(steps), width, text // 2), BF16)],
            flops=flops,
        )[0]

    near_steps = (0, 1, 3)
    send_across = context_terms(0, (2,), text_across)
    came_across = swap_tensor(send_across, 1)
    send = context_terms(0, near_steps, send_across)
    came = swap_tensor(send, 1)
    top, bottom = call(
        across_kernel,
        [where]
        + [(a, VMEM) for a in (low, wkv, came_across)]
        + [(send, ANY)],
        [((width // 2, text // 2), BF16)] * 2,
    )
    across = [send_x(top, 1), send_x(bottom, -1)]
    keep = context_terms(1, near_steps, top, flops=LONG)
    dq1, send1 = call(
        third_kernel,
        [where, (ds1, VMEM), (k, VMEM), (wq, VMEM), (keep, ANY)],
        [turned, pair],
    )
    came1 = swap_tensor(send1, 1)
    text_two, to_next, to_previous = call(
        x_add_kernel,
        [where] + [(a, VMEM) for a in (keep, came, *across, text_one, text_across)]
        + [(send1, ANY)],
        [((2,) + block, BF16)] + [((width, text // 2), BF16)] * 2,
        flops=LONG,
    )
    text_second = swap_z(text_two, 2)
    came_x = [send_x(to_next, 1), send_x(to_previous, -1)]

    keep1 = project(0, dq1, to_next)
    near1, far1 = call(
        meet_core_kernel,
        [where, (keep1, VMEM), (came1, VMEM)],
        [((width, rows), F32), turned],
    )
    others = (near1, swap_tensor(far1, 2))
    (sent,) = call(
        sent_kernel,
        [where, (sent0, VMEM), (g1, VMEM)] + [(a, VMEM) for a in others],
        [((2, rows, width), BF16)],
        [vm((2, rows, width), BF16), dma(1)],
        ANY,
    )

    few = text // NZ
    text_two, *by_z = call(
        z_add_kernel,
        [where] + [(a, VMEM) for a in (keep, came, *came_x, text_two)],
        [((2,) + block, BF16)] + [((few, width), BF16)] * (NZ // 2),
    )
    text_more = [from_z(text_two, 1), from_z(text_two, -1), text_second]
    came_z = [send_z(by_z[i], i) for i in range(NZ // 2)]
    context, context_low = call(
        z_sum_kernel,
        [where] + [(a, VMEM) for a in came_z] + [(text_second, ANY)],
        [((few, width), F32), ((few, width), BF16)],
    )
    context, context_low = call(
        core_sum_kernel,
        [where, (context, VMEM), (swap_tensor(context_low, 1), VMEM)],
        [((few, width), F32), ((few, width), BF16)],
    )
    far_context = swap_tensor(context_low, 2)
    tokens = few // NX
    (gathered,) = call(
        gather_kernel,
        [where] + [(a, VMEM) for a in (text_two, *text_more)],
        [((width, width), BF16)],
    )
    hidden, *to_send = call(
        text_kernel,
        [where] + [(a, VMEM) for a in (context, far_context, gathered)] + [(sent, HBM)],
        [((tokens, width), F32)] + [((tokens, width), BF16)] * (NX - 1),
        [vm((few, width), F32)],
    )
    for i, piece in enumerate(to_send):
        hidden = hidden + send_x(piece, i + 1).astype(F32)
    text_grad = hidden.T * gelu_slope(text_hidden.astype(F32))
    return (sent[None], text_grad)


def solution(mesh):
    placed = (
        P("section", "dp", "tensor"),
        P(None, "dp", "tensor"),
        P("section", None, "dp", "tensor"),
        P("section", "dp", "tensor"),
        P("section", "dp", "tensor"),
        P("section", None, "tensor"),
        P("section", None, "tensor"),
        P("section", None, "tensor"),
        P("section", "tensor"),
        P("tensor", ("dp", "section")),
    )
    return jax.shard_map(
        shards,
        mesh=mesh,
        in_specs=placed,
        out_specs=(P("section", None, "dp", "tensor"), P("tensor", ("dp", "section"))),
        check_vma=False,
    )
```
